128 devices in a mesh: ctx: 16 (over x_hi, z, core), head: 8 (over x_lo, y).
Axes of the slice: x: 4 (x_hi: 2, x_lo: 2; x = x_hi * 2 + x_lo), y: 4, z: 4, core: 2. Of those that a mesh axis runs over, the one named last changes fastest.
Arguments:
- coarse_query: bfloat16 [512, 3072], P(None, 'head'), may hold values from -5 to 5
- coarse_key: bfloat16 [512, 3072], P(None, 'head'), may hold values from -5 to 5
- coarse_value: bfloat16 [512, 3072], P(None, 'head'), may hold values from -5 to 5
- fine_query: bfloat16 [2048, 3072], P('ctx', 'head'), may hold values from -5 to 5
- fine_key: bfloat16 [2048, 3072], P('ctx', 'head'), may hold values from -5 to 5
- fine_value: bfloat16 [2048, 3072], P('ctx', 'head'), may hold values from -5 to 5
- coarse_sizes: int32 [6], replicated, may hold values from 1 to 128, 512 in all
- fine_sizes: int32 [6], replicated, may hold values from 1 to 512, 2048 in all
- fine_position: int32 [2048], P('ctx'), may hold values from 0 to 2047, as said below
- out_weight: bfloat16 [3072, 3072], P('head'), may hold values from -0.109375 to 0.109375
- coarse_cotangent: bfloat16 [512, 3072], P(None, 'head'), may hold values from -6 to 6
- fine_cotangent: bfloat16 [2048, 3072], P('ctx', 'head'), may hold values from -6 to 6
Outputs:
- coarse_out: bfloat16 [512, 3072], P(None, 'head')
- fine_out: bfloat16 [2048, 3072], P('ctx', 'head')
- coarse_dq: bfloat16 [512, 3072], P(None, 'head')
- coarse_dk: bfloat16 [512, 3072], P('ctx', 'head')
- coarse_dv: bfloat16 [512, 3072], P('ctx', 'head')
- fine_dq: bfloat16 [2048, 3072], P('ctx', 'head')
- fine_dk: bfloat16 [2048, 3072], P('ctx', 'head')
- fine_dv: bfloat16 [2048, 3072], P('ctx', 'head')
- out_weight_grad: float32 [3072, 3072], P('head', 'ctx')
The draws below stay inside these ranges and needn't reach their ends.
Inputs may be any that keep to these rules, and one draw needn't show every extreme that they name: `coarse_sizes`: the sizes sum to 512. `fine_sizes`: the sizes sum to 2048. `fine_position`: a permutation of 0 .. 2047; every aligned run of 64 rows holds consecutive positions in rising order.
All inputs are finite; a program needn't handle non-finite values.
Results may differ from the reference program's by a relative error of at most 0.04.
Values may be sent and summed in bfloat16 or wider, within the bound.
A program may use at most 128 MiB of HBM per device.

```python
import math
import jax
import jax.numpy as jnp
import numpy as np
from jax import lax

D = 3072
HEADS = 24
DH = 128
CSCALES = 6
FSCALES = 6
COARSE = 512
FINE_DEV = 128
FINE = 2048


def draw_coarse_query(key, part):
    key = jax.random.fold_in(key, 11)
    return jax.random.truncated_normal(key, -5.0, 5.0, (COARSE, HEADS * DH), jnp.float32).astype(jnp.bfloat16)


def draw_fine_query(key, part):
    key = jax.random.fold_in(key, 17)
    return jax.random.truncated_normal(key, -5.0, 5.0, (FINE, HEADS * DH), jnp.float32).astype(jnp.bfloat16)


def draw_coarse_key(key, part):
    key = jax.random.fold_in(key, 13)
    return jax.random.truncated_normal(key, -5.0, 5.0, (COARSE, HEADS * DH), jnp.float32).astype(jnp.bfloat16)


def draw_fine_position(key, part):
    key = jax.random.fold_in(key, 7)
    half_rows = FINE_DEV // 2
    order = jax.random.permutation(key, FINE // half_rows)
    return (order[:, None] * half_rows + jnp.arange(half_rows)[None, :]).reshape(FINE).astype(jnp.int32)


def spiked(values, stream_key, source, target, shards_of, factor):
    owner, partner = [(jnp.arange(values.shape[axis_at]) // (values.shape[axis_at] // shards_of)).reshape([-1 if axis == axis_at else 1 for axis in range(values.ndim)]) for axis_at in (source, target)]
    chosen = jax.random.permutation(stream_key, shards_of)[partner]
    strong = (owner == chosen) | (owner == (partner + shards_of // 2) % shards_of)
    return jnp.where(strong, factor * values, values)


def shard_levels(stream_key, extent, shards, least, high):
    def one(position, shards_of):
        draws = jax.random.uniform(jax.random.fold_in(jax.random.fold_in(stream_key, 6), position), (shards_of,), jnp.float32, least / len(shards), high / len(shards))
        return jnp.repeat(jnp.exp(draws), extent[position] // shards_of).reshape((-1,) + (1,) * (len(extent) - position - 1))

    level = one(*shards[0])
    for cut in shards[1:]:
        level = level * one(*cut)
    return level


def split_up(count, total, reach, slope):
    loads = [(1 << 20) // math.isqrt(grade ** slope) + 1 for grade in range(2, count + 1)]
    spare, holding = total - reach - (count - 1), [1] * (count - 1)
    while spare > 0:
        candidates = [i for i in range(count - 1) if holding[i] < reach]
        mass, budget = sum([loads[i] for i in candidates]), spare
        for i in candidates:
            more = min(reach - holding[i], max(1, budget * loads[i] // mass), spare)
            holding[i] = holding[i] + more
            spare = spare - more
    return np.array([reach] + holding)


def uneven_parts(key, count, total, reach, lean):
    if count == 2:
        one = jax.random.randint(key, (), max(1, total - reach), min(reach, total - 1) + 1)
        return jnp.stack([one, total - one])
    tallies = jnp.asarray(split_up(count, total, reach, lean), jnp.int32)
    twos = (count - 1) // 2
    donor, taker = tallies[1:1 + 2 * twos:2], tallies[2:2 + 2 * twos:2]
    margin = jnp.minimum(donor - 1, reach - taker)
    moved = jax.random.randint(jax.random.fold_in(key, 1), (twos,), 0, 1 << 20) % (margin + 1)
    tallies = tallies.at[1:1 + 2 * twos:2].set(donor - moved).at[2:2 + 2 * twos:2].set(taker + moved)
    return tallies[jax.random.permutation(jax.random.fold_in(key, 2), count)]


def scatter_about(own_key, shape, spread, limit, shards=(), held_as=jnp.bfloat16):
    loudness = shard_levels(own_key, shape, shards, -0.22, 0.18) if shards else 1.0
    array = jax.random.normal(own_key, shape, jnp.float32) * spread * loudness
    return jnp.minimum(jnp.maximum(array, -limit), limit).astype(held_as)


def noise_with(key, shape, spread, limit, shards, heavy, kind=jnp.bfloat16):
    array = spread * jax.random.normal(key, shape, jnp.float32)
    if shards:
        array = array * shard_levels(key, shape, shards, -0.22, 0.18)
    return jnp.clip(spiked(array, jax.random.fold_in(key, 3), *heavy), -limit, limit).astype(kind)


def setup_inputs(seed: int = 0) -> dict:
    arg_keys = jax.random.split(jax.random.key(seed), 13)
    return {
        "coarse_query": draw_coarse_query(jax.random.fold_in(arg_keys[12], 71), 0),
        "coarse_key": draw_coarse_key(jax.random.fold_in(arg_keys[12], 71), 0),
        "coarse_value": scatter_about(arg_keys[2], (COARSE, HEADS * DH), 1.0, 5.0, ((1, 8),)),
        "fine_query": draw_fine_query(jax.random.fold_in(arg_keys[12], 71), 0),
        "fine_key": scatter_about(arg_keys[4], (FINE, HEADS * DH), 1.0, 5.0, ((0, 16), (1, 8))),
        "fine_value": scatter_about(arg_keys[5], (FINE, HEADS * DH), 1.0, 5.0, ((0, 16), (1, 8))),
        "coarse_sizes": uneven_parts(arg_keys[6], CSCALES, COARSE, COARSE // 4, 2).astype(jnp.int32),
        "fine_sizes": uneven_parts(arg_keys[7], FSCALES, FINE, FINE // 4, 2).astype(jnp.int32),
        "fine_position": draw_fine_position(jax.random.fold_in(arg_keys[12], 71), 0),
        "out_weight": scatter_about(arg_keys[9], (HEADS * DH, D), (HEADS * DH) ** -0.5, 0.109375, ((0, 8),)),
        "coarse_cotangent": scatter_about(arg_keys[10], (COARSE, D), 1.0, 6.0, ((1, 8),)),
        "fine_cotangent": noise_with(arg_keys[11], (FINE, D), 1.0, 6.0, ((0, 16), (1, 8)), (0, 1, 16, 2.0)),
    }


NEGATIVE = -1e+30

def scale_ids(row_index, scale_sizes, first_scale):
    scale_ends = jnp.cumsum(scale_sizes)
    passed = (row_index[:, None] >= scale_ends[None, :]).astype(jnp.int32)
    return (first_scale + lax.optimization_barrier(jnp.sum(passed, axis=1))).astype(jnp.int32)

def reference(coarse_query, coarse_key, coarse_value, fine_query, fine_key, fine_value, coarse_sizes, fine_sizes, fine_position, out_weight, coarse_cotangent, fine_cotangent):
    factor = 1.0 / math.sqrt(DH)
    total_rows = COARSE + FINE
    block_width = min(512, COARSE)
    blocks = total_rows // block_width
    query = jnp.concatenate([coarse_query, fine_query], axis=0)
    key_rows = jnp.concatenate([coarse_key, fine_key], axis=0)
    value_rows = jnp.concatenate([coarse_value, fine_value], axis=0)
    cotangent = jnp.concatenate([coarse_cotangent, fine_cotangent], axis=0)
    row_scale = jnp.concatenate([scale_ids(jnp.arange(COARSE, dtype=jnp.int32), coarse_sizes, 0), scale_ids(fine_position, fine_sizes, CSCALES)])
    block_scale = row_scale.reshape(blocks, block_width)

    def head_columns(matrix, head_index):
        return lax.dynamic_slice_in_dim(matrix, (head_index * DH).astype(jnp.int32), DH, 1)

    def masked_scores(query_block, key_head, query_scale):
        raw_scores = jnp.dot(query_block, key_head.T, preferred_element_type=jnp.float32) * factor
        allowed = row_scale[None, :] <= query_scale[:, None]
        return (jnp.where(allowed, raw_scores, NEGATIVE), allowed)

    def forward_head(head_index):
        key_head = head_columns(key_rows, head_index)
        value_head = head_columns(value_rows, head_index)
        query_blocks = head_columns(query, head_index).reshape(blocks, block_width, DH)

        def one_block(inputs):
            query_block, query_scale = inputs
            scores, allowed = masked_scores(query_block, key_head, query_scale)
            highest = lax.optimization_barrier(jnp.max(scores, axis=1))
            totals = lax.optimization_barrier(jnp.sum(jnp.where(allowed, jnp.exp(scores - highest[:, None]), 0.0), axis=1))
            log_sums = highest + jnp.log(totals)
            weights = jnp.where(allowed, jnp.exp(scores - log_sums[:, None]), 0.0).astype(jnp.bfloat16)
            attn_block = jnp.dot(weights, value_head, preferred_element_type=jnp.float32).astype(jnp.bfloat16)
            return (attn_block, log_sums)
        attn_blocks, log_blocks = lax.map(one_block, (query_blocks, block_scale))
        return (attn_blocks.reshape(total_rows, DH), log_blocks.reshape(total_rows))
    attn_heads, log_heads = lax.map(forward_head, jnp.arange(HEADS, dtype=jnp.int32))
    attn = attn_heads.transpose(1, 0, 2).reshape(total_rows, HEADS * DH)
    outputs = jnp.dot(attn, out_weight, preferred_element_type=jnp.float32).astype(jnp.bfloat16)
    grad_attn = jnp.dot(cotangent, out_weight.T, preferred_element_type=jnp.float32).astype(jnp.bfloat16)
    out_weight_grad = jnp.dot(attn.T, cotangent, preferred_element_type=jnp.float32)

    def backward_head(head_index):
        key_head = head_columns(key_rows, head_index)
        value_head = head_columns(value_rows, head_index)
        query_head = head_columns(query, head_index)
        grad_head = head_columns(grad_attn, head_index)
        attn_head = head_columns(attn, head_index)
        deltas = lax.optimization_barrier(jnp.sum(grad_head.astype(jnp.float32) * attn_head.astype(jnp.float32), axis=1))

        def one_block(running, inputs):
            key_sum, value_sum = running
            query_block, grad_block, query_scale, log_block, delta_block = inputs
            scores, allowed = masked_scores(query_block, key_head, query_scale)
            unrounded = jnp.where(allowed, jnp.exp(scores - log_block[:, None]), 0.0)
            grad_probs = jnp.dot(grad_block, value_head.T, preferred_element_type=jnp.float32)
            grad_scores = (unrounded * (grad_probs - delta_block[:, None]) * factor).astype(jnp.bfloat16)
            query_grad = jnp.dot(grad_scores, key_head, preferred_element_type=jnp.float32).astype(jnp.bfloat16)
            key_sum = key_sum + jnp.dot(grad_scores.T, query_block, preferred_element_type=jnp.float32)
            value_sum = value_sum + jnp.dot(unrounded.astype(jnp.bfloat16).T, grad_block, preferred_element_type=jnp.float32)
            return ((key_sum, value_sum), query_grad)
        zero_rows = jnp.zeros((total_rows, DH), jnp.float32)
        inputs = (query_head.reshape(blocks, block_width, DH), grad_head.reshape(blocks, block_width, DH), block_scale, log_heads[head_index].reshape(blocks, block_width), deltas.reshape(blocks, block_width))
        sums, query_grad = lax.scan(one_block, (zero_rows, zero_rows), inputs)
        return (query_grad.reshape(total_rows, DH), sums[0].astype(jnp.bfloat16), sums[1].astype(jnp.bfloat16))
    query_grads, key_grads, value_grads = lax.map(backward_head, jnp.arange(HEADS, dtype=jnp.int32))

    def merge_heads(stacked):
        return stacked.transpose(1, 0, 2).reshape(total_rows, HEADS * DH)
    query_grads = merge_heads(query_grads)
    key_grads = merge_heads(key_grads)
    value_grads = merge_heads(value_grads)
    return (outputs[:COARSE], outputs[COARSE:], query_grads[:COARSE], key_grads[:COARSE], value_grads[:COARSE], query_grads[COARSE:], key_grads[COARSE:], value_grads[COARSE:], out_weight_grad)
```

```python
import math

import jax
import jax.numpy as jnp
from jax import lax
from jax.experimental import pallas as pl
from jax.experimental.pallas import tpu as pltpu
from jax.sharding import PartitionSpec as P

DH = 128
HL = 3
FR = 128
CR = 32
R = FR + CR
KR = 272
CH = 512
NEG = -1e30
BF = jnp.bfloat16
F32 = jnp.float32
MESH = pl.DeviceIdType.MESH
NT = (((1,), (1,)), ((), ()))
TN = (((0,), (0,)), ((), ()))
NN = (((1,), (0,)), ((), ()))


def dot(a, b, dims):
    return lax.dot_general(a, b, dims, preferred_element_type=F32)


def ctx_of(slot):
    core, rest = divmod(slot, 8)
    z, xh = divmod(rest, 2)
    return (xh * 4 + z) * 2 + core


def kernel(
    cq, ck, cv, fq, fk, fv, csz, fsz, fpos, w, cc, fc,
    cout, fout, cdq, cdk, cdv, fdq, fdk, fdv, wg,
    qs, kv, cotb, ksc, tbuf, ebuf, attn_s, do_s,
    part, sibr, ra, rb, r1, r3, rx,
    opart, ora, orb, or1, or3, orx, fbuf, wsend, wrecv,
    ssem, rsem,
):
    ctx = lax.axis_index("ctx")
    head = lax.axis_index("head")
    core = ctx % 2
    z = (ctx // 2) % 4
    xh = ctx // 8
    y = head % 4
    xl = head // 4
    z1 = z + 1 - 2 * (z % 2)
    z3 = 3 - z
    z2 = (z + 2) % 4
    y1 = y + 1 - 2 * (y % 2)
    y3 = 3 - y
    y2 = (y + 2) % 4

    def ctx_id(a, b, c):
        return ((a * 4 + b) * 2 + c, head)

    sib = ctx_id(xh, z, 1 - core)
    px = ctx_id(1 - xh, z, core)
    pz1 = ctx_id(xh, z1, core)
    pz3 = ctx_id(xh, z3, core)
    py1 = (ctx, xl * 4 + y1)
    py3 = (ctx, xl * 4 + y3)
    pxl = (ctx, (1 - xl) * 4 + y)
    peers = (sib, px, pz1, pz3, py1, py3, pxl)

    count = [0]
    started = []

    def send(src, dst, peer):
        i = count[0]
        count[0] += 1
        copy = pltpu.make_async_remote_copy(
            src_ref=src,
            dst_ref=dst,
            send_sem=ssem.at[i],
            recv_sem=rsem.at[i],
            device_id=peer,
            device_id_type=MESH,
        )
        copy.start()
        started.append(copy)
        return copy

    iota_l = lax.broadcasted_iota(jnp.int32, (1, 128), 1)

    def scale_of(position, sizes, first):
        end = jnp.int32(0)
        total = jnp.zeros(position.shape, jnp.int32) + first
        for s in range(6):
            end = end + sizes[s]
            total = total + (position >= end).astype(jnp.int32)
        return total.astype(F32)

    fsc_row = scale_of(fpos[...], fsz, 6)
    own = core * 8 + z * 2 + xh
    for h in range(HL):
        hs = pl.ds(h * DH, DH)
        kv[h, own, 0:128, :] = fk[:, hs]
        kv[h, own, 128:256, :] = fv[:, hs]
        kv[h, own, 256:272, :] = jnp.broadcast_to(fsc_row, (16, 128)).astype(BF)
    cotb[y * 2 + xl, 0:FR, :] = fc[...]
    cotb[y * 2 + xl, FR:R, :] = cc[pl.ds(pl.multiple_of(ctx * CR, CR), CR), :]

    barrier = pltpu.get_barrier_semaphore()
    for peer in peers:
        pl.semaphore_signal(barrier, inc=1, device_id=peer, device_id_type=MESH)
    pl.semaphore_wait(barrier, len(peers))

    class Gather:
        def __init__(self, at, split, pair, ring, ring1, ring3, first, ids, sibling):
            self.at, self.split = at, split
            self.pair, self.ring, self.ring1, self.ring3, self.first = pair, ring, ring1, ring3, first
            self.ids, self.sibling = ids, sibling

        def a(self):
            v = self.at(self.first + self.ring * 2 + self.pair, 1, None)
            self.cx = send(v, v, self.ids[0])

        def b(self):
            self.cx.wait_recv()
            v = self.at(self.first + self.ring * 2, 2, None)
            self.c1 = send(v, v, self.ids[1])
            self.c3 = send(v, v, self.ids[2])

        def c(self):
            self.c1.wait_recv()
            v = self.at(self.first + self.ring1 * 2, 2, 0)
            self.ca = send(v, v, self.ids[2])
            self.c3.wait_recv()
            v = self.at(self.first + self.ring3 * 2, 2, 1)
            self.cb = send(v, v, self.ids[1])

        def d(self):
            self.ca.wait_recv()
            self.cb.wait_recv()
            if self.sibling is not None:
                v = self.at(self.first, 8, None)
                self.cs = send(v, v, self.sibling)

        def e(self):
            if self.sibling is not None:
                self.cs.wait_recv()

    ctx_ids = (px, pz1, pz3)
    head_ids = (pxl, py1, py3)

    def rows_at(ref, cut, total):
        def at(slot, n, half):
            if half is None:
                return ref.at[pl.ds(slot, n)]
            return ref.at[pl.ds(slot, n), pl.ds(0, cut) if half == 0 else pl.ds(cut, total - cut)]

        return at

    gathers = [
        Gather(rows_at(kv.at[h], 128, KR), None, xh, z, z1, z3, core * 8, ctx_ids, sib)
        for h in range(HL)
    ]
    cot_gather = Gather(rows_at(cotb, 80, R), None, xl, y, y1, y3, 0, head_ids, None)

    gathers[0].a()
    cot_gather.a()
    gathers[1].a()
    gathers[2].a()

    for h in range(HL):
        hs = pl.ds(h * DH, DH)
        qs[h, 0:FR, :] = fq[:, hs]
        qs[h, FR:R, :] = cq[pl.ds(pl.multiple_of(ctx * CR, CR), CR), hs]
    diag = lax.broadcasted_iota(jnp.int32, (128, 128), 0) == lax.broadcasted_iota(
        jnp.int32, (128, 128), 1
    )
    fsc_col = jnp.sum(jnp.where(diag, jnp.broadcast_to(fsc_row, (128, 128)), 0.0), axis=1, keepdims=True)
    csc_col = scale_of(lax.broadcasted_iota(jnp.int32, (CR, 1), 0) + ctx * CR, csz, 0)
    qsc = jnp.concatenate([fsc_col, csc_col], axis=0)
    ksc[:, 0:512] = scale_of(lax.broadcasted_iota(jnp.int32, (8, 512), 1), csz, 0)

    gathers[0].b()
    cot_gather.b()
    gathers[1].b()
    gathers[2].b()
    gathers[0].c()
    cot_gather.c()
    gathers[0].d()
    gathers[1].c()
    cot_gather.d()
    gathers[2].c()
    gathers[0].e()
    for slot in range(16):
        ksc[:, 512 + slot * 128 : 640 + slot * 128] = kv[0, slot, 256:272, :].astype(F32)[0:8]

    to_log2 = math.log2(math.e) / math.sqrt(DH)
    factor = 1.0 / math.sqrt(DH)

    def key_block(h, j):
        if j == 0:
            return ck[:, h * DH : (h + 1) * DH]
        return kv[h, 4 * (j - 1) : 4 * j, 0:128, :].reshape(512, DH)

    def value_block(h, j):
        if j == 0:
            return cv[:, h * DH : (h + 1) * DH]
        return kv[h, 4 * (j - 1) : 4 * j, 128:256, :].reshape(512, DH)

    inverse = [None] * HL

    def forward(h):
        q = qs[h]
        high = None
        for j in range(5):
            cols = slice(512 * j, 512 * (j + 1))
            s = dot(q, key_block(h, j), NT) * to_log2
            s = jnp.where(ksc[0:1, cols] <= qsc, s, NEG)
            tbuf[:, cols] = s
            top = jnp.max(s, axis=1, keepdims=True)
            high = top if high is None else jnp.maximum(high, top)
        total = jnp.zeros((R, 1), F32)
        acc = jnp.zeros((R, DH), F32)
        for j in range(5):
            cols = slice(512 * j, 512 * (j + 1))
            e = jnp.exp2(tbuf[:, cols] - high)
            total = total + jnp.sum(e, axis=1, keepdims=True)
            eb = e.astype(BF)
            ebuf[h, :, cols] = eb
            acc = acc + dot(eb, value_block(h, j), NN)
        inverse[h] = 1.0 / total
        attn_s[:, h * DH : (h + 1) * DH] = (acc * inverse[h]).astype(BF)

    def grad_attn():
        acc = jnp.zeros((R, HL * DH), F32)
        for slot in range(8):
            block = (slot % 2) * 4 + slot // 2
            acc = acc + dot(cotb[slot], w[:, block * 384 : (block + 1) * 384], NT)
        do_s[...] = acc.astype(BF)

    def weight_grad(h):
        a_t = attn_s[:, h * DH : (h + 1) * DH].astype(F32).T.astype(BF)
        for slot in range(8):
            g = dot(a_t, cotb[slot], NN).astype(BF)
            for half in range(2):
                for i in range(3):
                    part[h, half * 8 + slot, 320 + 64 * i : 384 + 64 * i, :] = g[
                        64 * half : 64 * half + 64, 128 * i : 128 * i + 128
                    ]

    def backward(h):
        cols_h = slice(h * DH, (h + 1) * DH)
        go = do_s[:, cols_h]
        gof = go.astype(F32)
        delta = jnp.sum(gof * attn_s[:, cols_h].astype(F32), axis=1, keepdims=True)
        c = inverse[h] * factor
        go_t = (gof * inverse[h]).T.astype(BF)
        q_t = qs[h].astype(F32).T.astype(BF)
        dq = jnp.zeros((R, DH), F32)
        for j in range(5):
            cols = slice(512 * j, 512 * (j + 1))
            dp = dot(go, value_block(h, j), NT)
            eb = ebuf[h, :, cols]
            ds = (eb.astype(F32) * ((dp - delta) * c)).astype(BF)
            dq = dq + dot(ds, key_block(h, j), NN)
            dk_t = dot(q_t, ds, NN)
            dv_t = dot(go_t, eb, NN)
            if j == 0:
                dk = dk_t.T.astype(BF)
                dv = dv_t.T.astype(BF)
                for slot in range(16):
                    at = ctx_of(slot) * CR
                    part[h, slot, 256:288, :] = dk[at : at + CR]
                    part[h, slot, 288:320, :] = dv[at : at + CR]
            else:
                for i in range(4):
                    slot = 4 * (j - 1) + i
                    part[h, slot, 0:128, :] = dk_t[:, 128 * i : 128 * i + 128].astype(BF)
                    part[h, slot, 128:256, :] = dv_t[:, 128 * i : 128 * i + 128].astype(BF)
        dqb = dq.astype(BF)
        fdq[:, cols_h] = dqb[0:FR]
        fbuf[pl.ds(own, 1), CR : 2 * CR, cols_h] = dqb[FR:R][None]

    class Scatter:
        def __init__(self, src, sibling, bufs, cut, pair, ring, ring1, ring2, ring3, first, ids):
            self.src, self.sibling, self.bufs, self.cut = src, sibling, bufs, cut
            self.pair, self.ring, self.ring1, self.ring2, self.ring3 = pair, ring, ring1, ring2, ring3
            self.first, self.ids = first, ids
            self.rows = src.shape[1]

        def add(self, slot, half, other):
            rows = pl.ds(0, self.cut) if half == 0 else pl.ds(self.cut, self.rows - self.cut)
            if half is None:
                rows = pl.ds(0, self.rows)
            v = self.src.at[pl.ds(slot, 2), rows]
            v[...] = (v[...].astype(F32) + other[...].astype(F32)).astype(BF)

        def a(self):
            if self.sibling is not None:
                peer, landing = self.sibling
                self.cs = send(self.src.at[pl.ds(8 - self.first, 8)], landing, peer)

        def b(self):
            if self.sibling is not None:
                self.cs.wait_recv()
                landing = self.sibling[1]
                for r in (self.ring2, self.ring1, self.ring3, self.ring):
                    self.add(self.first + r * 2, None, landing.at[pl.ds(r * 2, 2)])
                    if r is self.ring2:
                        self.send_far()
            else:
                self.send_far()

        def send_far(self):
            far = self.src.at[pl.ds(self.first + self.ring2 * 2, 2)]
            ta, tb = self.bufs[0], self.bufs[1]
            self.ca = send(far.at[:, pl.ds(0, self.cut)], ta, self.ids[1])
            self.cb = send(far.at[:, pl.ds(self.cut, self.rows - self.cut)], tb, self.ids[2])

        def c(self):
            self.ca.wait_recv()
            self.add(self.first + self.ring3 * 2, 0, self.bufs[0])
            self.c3 = send(self.src.at[pl.ds(self.first + self.ring3 * 2, 2)], self.bufs[3], self.ids[2])
            self.cb.wait_recv()
            self.add(self.first + self.ring1 * 2, 1, self.bufs[1])
            self.c1 = send(self.src.at[pl.ds(self.first + self.ring1 * 2, 2)], self.bufs[2], self.ids[1])

        def d(self):
            self.c1.wait_recv()
            self.c3.wait_recv()
            o = self.first + self.ring * 2
            other = 1 - self.pair

            def summed(p):
                return (
                    self.src[pl.ds(o + p, 1)].astype(F32)
                    + self.bufs[2][pl.ds(p, 1)].astype(F32)
                    + self.bufs[3][pl.ds(p, 1)].astype(F32)
                )

            self.src[pl.ds(o + other, 1)] = summed(other).astype(BF)
            self.cx = send(self.src.at[o + other], self.bufs[4], self.ids[0])
            self.mine = summed(self.pair)[0]

        def e(self):
            self.cx.wait_recv()
            return self.mine + self.bufs[4][...].astype(F32)

    scatters = [
        Scatter(
            part.at[h],
            (sib, sibr.at[h]),
            (ra.at[h], rb.at[h], r1.at[h], r3.at[h], rx.at[h]),
            256, xh, z, z1, z2, z3, core * 8, ctx_ids,
        )
        for h in range(HL)
    ]
    out_scatter = Scatter(
        opart, None, (ora, orb, or1, or3, orx), 80, xl, y, y1, y2, y3, 0, head_ids
    )

    forward(0)
    gathers[1].d()
    gathers[2].d()
    grad_attn()
    weight_grad(0)
    backward(0)
    scatters[0].a()
    gathers[1].e()
    forward(1)
    scatters[0].b()
    weight_grad(1)
    backward(1)
    scatters[0].c()
    scatters[1].a()
    gathers[2].e()
    forward(2)
    scatters[1].b()
    for slot in range(8):
        block = (slot % 2) * 4 + slot // 2
        opart[slot] = dot(attn_s[...], w[:, block * 384 : (block + 1) * 384], NN).astype(BF)
    out_scatter.b()
    weight_grad(2)
    scatters[0].d()
    backward(2)
    scatters[2].a()
    scatters[1].c()
    out_scatter.c()
    scatters[2].b()
    out_scatter.d()

    lane = lax.broadcasted_iota(jnp.int32, (64, 128), 1)

    def finish(h):
        total = scatters[h].e()
        cols_h = slice(h * DH, (h + 1) * DH)
        fdk[:, cols_h] = total[0:128].T.astype(BF)
        fdv[:, cols_h] = total[128:256].T.astype(BF)
        cdk[:, cols_h] = total[256:288].astype(BF)
        cdv[:, cols_h] = total[288:320].astype(BF)
        c0, c1, c2 = total[320:384], total[384:448], total[448:512]
        s1 = pltpu.roll(c1, 64, 1)
        s2 = pltpu.roll(c2, 64, 1)
        b0 = jnp.where(lane < 64, s1, s2)
        zero = core == 0
        keep0 = jnp.where(zero, c0, b0)
        keep1 = jnp.where(zero, c1, s2)
        wsend[h, :, 0:128] = jnp.where(zero, b0, c0)
        wsend[h, :, 128:256] = jnp.where(zero, s2, c1)
        rows = pl.ds(pl.multiple_of(h * DH + core * 64, 64), 64)
        wg[rows, 0:128] = keep0
        wg[rows, 128:192] = keep1[:, 0:64]
        return send(wsend.at[h], wrecv.at[h], sib)

    total = out_scatter
    w0 = finish(0)
    out_rows = total.e().astype(BF)
    fout[...] = out_rows[0:FR]
    fbuf[pl.ds(own, 1), 0:CR, :] = out_rows[FR:R][None]
    last = Gather(rows_at(fbuf, 32, 64), None, xh, z, z1, z3, core * 8, ctx_ids, sib)
    last.a()
    scatters[1].d()
    scatters[2].c()
    last.b()
    last.c()
    w1 = finish(1)
    scatters[2].d()
    last.d()
    w2 = finish(2)
    last.e()
    for slot in range(16):
        at = ctx_of(slot) * CR
        cout[at : at + CR, :] = fbuf[slot, 0:CR, :]
        cdq[at : at + CR, :] = fbuf[slot, CR : 2 * CR, :]
    for h, cw in enumerate((w0, w1, w2)):
        cw.wait_recv()
        rows = pl.ds(pl.multiple_of(h * DH + (1 - core) * 64, 64), 64)
        wg[rows, 0:128] = wrecv[h, :, 0:128]
        wg[rows, 128:192] = wrecv[h, :, 128:192]
    for copy in started:
        copy.wait_send()


def on_device(cq, ck, cv, fq, fk, fv, csz, fsz, fpos, w, cc, fc):
    vmem = pl.BlockSpec(memory_space=pltpu.VMEM)
    smem = pl.BlockSpec(memory_space=pltpu.SMEM)
    shapes = [
        ((512, 384), BF), ((128, 384), BF), ((512, 384), BF), ((32, 384), BF), ((32, 384), BF),
        ((128, 384), BF), ((128, 384), BF), ((128, 384), BF), ((384, 192), F32),
    ]
    v = pltpu.VMEM
    return pl.pallas_call(
        kernel,
        out_shape=[jax.ShapeDtypeStruct(s, d) for s, d in shapes],
        in_specs=[vmem] * 6 + [smem] * 2 + [vmem] * 4,
        out_specs=[vmem] * 9,
        scratch_shapes=[
            v((HL, R, DH), BF),
            v((HL, 16, KR, DH), BF),
            v((8, R, 384), BF),
            v((8, 2560), F32),
            v((R, 2560), F32),
            v((HL, R, 2560), BF),
            v((R, 384), BF),
            v((R, 384), BF),
            v((HL, 16, CH, DH), BF),
            v((HL, 8, CH, DH), BF),
            v((HL, 2, CH // 2, DH), BF),
            v((HL, 2, CH // 2, DH), BF),
            v((HL, 2, CH, DH), BF),
            v((HL, 2, CH, DH), BF),
            v((HL, CH, DH), BF),
            v((8, R, 384), BF),
            v((2, 80, 384), BF),
            v((2, 80, 384), BF),
            v((2, R, 384), BF),
            v((2, R, 384), BF),
            v((R, 384), BF),
            v((16, 2 * CR, 384), BF),
            v((HL, 64, 256), F32),
            v((HL, 64, 256), F32),
            pltpu.SemaphoreType.DMA((64,)),
            pltpu.SemaphoreType.DMA((64,)),
        ],
        compiler_params=pltpu.CompilerParams(
            collective_id=0, has_side_effects=True, vmem_limit_bytes=56 * 2**20
        ),
        cost_estimate=pl.CostEstimate(flops=7 * 10**9, bytes_accessed=8 * 10**6, transcendentals=1300000),
    )(cq, ck, cv, fq, fk, fv, csz, fsz, fpos.reshape(1, 128), w, cc, fc)


def solution(mesh):
    placed = (
        P(None, "head"), P(None, "head"), P(None, "head"),
        P("ctx", "head"), P("ctx", "head"), P("ctx", "head"),
        P(), P(), P("ctx"), P("head", None), P(None, "head"), P("ctx", "head"),
    )
    return jax.shard_map(
        on_device,
        mesh=mesh,
        in_specs=placed,
        out_specs=(
            P(None, "head"), P("ctx", "head"), P(None, "head"),
            P("ctx", "head"), P("ctx", "head"), P("ctx", "head"),
            P("ctx", "head"), P("ctx", "head"), P("head", "ctx"),
        ),
        check_vma=False,
    )
```

```python
import math

import jax
import jax.numpy as jnp
from jax import lax
from jax.experimental import pallas as pl
from jax.experimental.pallas import tpu as pltpu
from jax.sharding import PartitionSpec as P

DH = 128
HL = 3
FR = 128
CR = 32
R = FR + CR
KR = 272
CA = 320
CW = 192
HALF = 256
NEG = -1e30
BF = jnp.bfloat16
F32 = jnp.float32
MESH = pl.DeviceIdType.MESH
NT = (((1,), (1,)), ((), ()))
TN = (((0,), (0,)), ((), ()))
NN = (((1,), (0,)), ((), ()))


def dot(a, b, dims):
    return lax.dot_general(a, b, dims, preferred_element_type=F32)


def kernel(
    cq, ck_in, cv_in, fq, fk, fv, csz, fsz, fpos, w_in, cc, fc,
    fout_o, fdq_o, fdk_o, fdv_o, cdk_o, cdv_o, wg_o, obuf_o, qbuf_o,
    ck, cv, w, q2, qc, kv, cotb, scx, ksc, tbuf, ebuf, ecds, ecx, attn_all, do_c, gcn, gcx, do2,
    on_s, on_r, st_s, st_r, dq_s, dq_r,
    pa, pw, sa, sw, az, wz, wx,
    oc, ocr, ocx, of, ofr, ofx, obuf, qbuf, wsend, wrecv,
    fout, fdq, fdk, fdv, cdk, cdv, wg,
    ssem, rsem, isem, osem,
):
    ctx = lax.axis_index("ctx")
    head = lax.axis_index("head")
    core = ctx % 2
    z = (ctx // 2) % 4
    xh = ctx // 8
    y = head % 4
    xl = head // 4
    z1 = z + 1 - 2 * (z % 2)
    z3 = 3 - z
    z2 = (z + 2) % 4
    y1 = y + 1 - 2 * (y % 2)
    y3 = 3 - y
    y2 = (y + 2) % 4

    def ctx_id(a, b, c):
        return ((a * 4 + b) * 2 + c, head)

    sib = ctx_id(xh, z, 1 - core)
    px = ctx_id(1 - xh, z, core)
    pz1 = ctx_id(xh, z1, core)
    pz3 = ctx_id(xh, z3, core)
    py1 = (ctx, xl * 4 + y1)
    py3 = (ctx, xl * 4 + y3)
    py2 = (ctx, xl * 4 + y2)
    pz2 = ctx_id(xh, z2, core)
    pxl = (ctx, (1 - xl) * 4 + y)
    peers = (px, pz2, pz3, pz1, py2, py3, py1, pxl, sib)

    barrier = pltpu.get_barrier_semaphore()
    for peer in peers:
        pl.semaphore_signal(barrier, inc=1, device_id=peer, device_id_type=MESH)

    loads = [0]

    def load(src, dst):
        copy = pltpu.make_async_copy(src, dst, isem.at[loads[0]])
        loads[0] += 1
        copy.start()
        return copy

    share = pl.ds(pl.multiple_of(ctx * CR, CR), CR)
    pair_share = pl.ds(pl.multiple_of((((1 - xh) * 4 + z) * 2 + core) * CR, CR), CR)
    in_kv = []
    for h in range(HL):
        hs = pl.ds(h * DH, DH)
        in_kv.append((load(fk.at[:, hs], kv.at[h, core, z, pl.ds(0, 128)]), load(fv.at[:, hs], kv.at[h, core, z, pl.ds(128, 128)])))
        if h == 0:
            in_cot = (load(fc, cotb.at[y, xl, pl.ds(0, FR)]), load(cc.at[share], cotb.at[y, xl, pl.ds(FR, CR)]))
    in_q = []
    for h in range(HL):
        hs = pl.ds(h * DH, DH)
        in_q.append((load(fq.at[:, hs], q2.at[h, pl.ds(0, FR)]), load(cq.at[share, hs], qc.at[h, pl.ds(0, CR)]), load(cq.at[pair_share, hs], qc.at[h, pl.ds(CR, CR)])))
    in_ck = load(ck_in, ck)
    in_cv = load(cv_in, cv)
    in_w = load(w_in, w)

    def scale_of(position, sizes, first):
        end = jnp.int32(0)
        total = jnp.zeros(position.shape, jnp.int32) + first
        for s in range(6):
            end = end + sizes[s]
            total = total + (position >= end).astype(jnp.int32)
        return total.astype(F32)

    fsc_row = scale_of(fpos[...], fsz, 6)
    for h in range(HL):
        kv[h, core, z, 256:272, :] = jnp.broadcast_to(fsc_row, (16, 128)).astype(BF)

    count = [0]
    started = []

    def send(src, dst, peer):
        i = count[0]
        count[0] += 1
        copy = pltpu.make_async_remote_copy(
            src_ref=src,
            dst_ref=dst,
            send_sem=ssem.at[i],
            recv_sem=rsem.at[i],
            device_id=peer,
            device_id_type=MESH,
        )
        copy.start()
        started.append(copy)
        return copy

    rings = (z2, z1, z3)
    pz = (pz2, pz1, pz3)
    py = (py2, py1, py3)

    class Gather:
        def __init__(self, at, all_of, ring, pair, ids, pair_id, sibling):
            self.at, self.all_of, self.ring, self.pair = at, all_of, ring, pair
            self.ids, self.pair_id, self.sibling = ids, pair_id, sibling

        def a(self):
            v = self.at(self.ring, self.pair)
            if self.pair_id is not None:
                self.cx = send(v, v, self.pair_id)
            self.waits = [send(v, v, peer) for peer in self.ids]

        def b(self):
            self.cx.wait_recv()
            v = self.at(self.ring, 1 - self.pair)
            self.waits += [send(v, v, peer) for peer in self.ids]

        def d(self):
            for copy in self.waits:
                copy.wait_recv()
            if self.sibling is not None:
                self.cs = send(self.all_of, self.all_of, self.sibling)

        def e(self):
            self.cs.wait_recv()

    gathers = [
        Gather((lambda h: lambda r, p: kv.at[h, core, r])(h), kv.at[h, core], z, None, pz, None, sib)
        for h in range(HL)
    ]
    cot_gather = Gather(lambda r, p: cotb.at[r, p], None, y, xl, py, pxl, None)
    out_gather = Gather(lambda r, p: obuf.at[core, r, p], obuf.at[core], z, xh, pz, px, sib)
    dq_gather = Gather(lambda r, p: qbuf.at[core, r, p], qbuf.at[core], z, xh, pz, px, sib)

    pl.semaphore_wait(barrier, len(peers))

    def gather_a(h):
        for copy in in_kv[h]:
            copy.wait()
        gathers[h].a()

    for copy in in_cot:
        copy.wait()
    cot_gather.a()
    gather_a(0)
    for copy in in_q[0] + in_q[1] + in_q[2]:
        copy.wait()
    own_rows, pair_rows = pl.ds(0, FR), pl.ds(FR, FR)
    c_scale = send(kv.at[0, core, z, pl.ds(256, 16)], scx, px)
    c_query = send(q2.at[:, own_rows], q2.at[:, pair_rows], px)

    diag = lax.broadcasted_iota(jnp.int32, (128, 128), 0) == lax.broadcasted_iota(
        jnp.int32, (128, 128), 1
    )

    def column(row):
        return jnp.sum(jnp.where(diag, jnp.broadcast_to(row, (128, 128)), 0.0), axis=1, keepdims=True)

    fsc_col = column(fsc_row)
    csc_col = scale_of(lax.broadcasted_iota(jnp.int32, (CR, 1), 0) + ctx * CR, csz, 0)
    csc_row = scale_of(lax.broadcasted_iota(jnp.int32, (1, 512), 1), csz, 0)

    to_log2 = math.log2(math.e) / math.sqrt(DH)
    factor = 1.0 / math.sqrt(DH)
    planes = (1 - core, core)

    blocks = (slice(0, 256), slice(256, 768), slice(768, 1280))
    half_rows = pl.ds(pl.multiple_of(xh * HALF, HALF), HALF)

    def key_block(h, j):
        if j == 0:
            return ck[half_rows, h * DH : (h + 1) * DH]
        return kv[h, planes[j - 1], :, 0:128, :].reshape(512, DH)

    def value_block(h, j):
        if j == 0:
            return cv[half_rows, h * DH : (h + 1) * DH]
        return kv[h, planes[j - 1], :, 128:256, :].reshape(512, DH)

    inverse = [None] * HL
    inverse_c = [None] * HL
    high = [None] * HL
    total = [None] * HL
    row_scale = [None]

    def coarse_forward(h):
        cols_h = slice(h * DH, (h + 1) * DH)
        s = dot(qc[h, 0:CR, :], ck[:, cols_h], NT) * to_log2
        s = jnp.where(csc_row <= csc_col, s, NEG)
        e = jnp.exp2(s - jnp.max(s, axis=1, keepdims=True))
        inverse_c[h] = 1.0 / jnp.sum(e, axis=1, keepdims=True)
        eb = e.astype(BF)
        for i in range(2):
            ecds[h, i, 0] = eb[:, HALF * i : HALF * (i + 1)]
        acc = dot(eb, cv[:, cols_h], NN)
        attn_all[FR:R, cols_h] = (acc * inverse_c[h]).astype(BF)

    def forward(h):
        m = None
        for j, cols in enumerate(blocks):
            s = dot(q2[h], key_block(h, j), NT) * to_log2
            if j > 0:
                s = jnp.where(ksc[0:1, cols.start - 256 : cols.stop - 256] <= row_scale[0], s, NEG)
            tbuf[h, :, cols] = s
            top = jnp.max(s, axis=1, keepdims=True)
            m = top if m is None else jnp.maximum(m, top)
        l = jnp.zeros((2 * FR, 1), F32)
        acc = jnp.zeros((2 * FR, DH), F32)
        for j, cols in enumerate(blocks):
            e = jnp.exp2(tbuf[h, :, cols] - m)
            l = l + jnp.sum(e, axis=1, keepdims=True)
            eb = e.astype(BF)
            ebuf[h, :, cols] = eb
            acc = acc + dot(eb, value_block(h, j), NN)
        high[h], total[h] = m, l
        on_s[h] = (acc * (1.0 / l)).astype(BF)
        lane2 = lax.broadcasted_iota(jnp.int32, (2 * FR, 128), 1)
        st_s[h] = jnp.where(lane2 == 0, m, l).T[0:8]
        return send(on_s.at[h], on_r.at[h], px), send(st_s.at[h], st_r.at[h], px)

    def swapped(v):
        return jnp.concatenate([v[FR:], v[:FR]], axis=0)

    def combine(h, copies):
        for copy in copies:
            copy.wait_recv()
        st = swapped(jnp.concatenate([st_r[h]] * 16, axis=0).T)
        m2, l2 = st[:, 0:1], st[:, 1:2]
        m1, l1 = high[h], total[h]
        m = jnp.maximum(m1, m2)
        f1 = jnp.exp2(m1 - m)
        w1, w2 = l1 * f1, l2 * jnp.exp2(m2 - m)
        rl = 1.0 / (w1 + w2)
        inverse[h] = f1 * rl
        both = on_s[h].astype(F32) * (w1 * rl) + swapped(on_r[h].astype(F32)) * (w2 * rl)
        both = both.astype(BF)
        cols_h = slice(h * DH, (h + 1) * DH)
        attn_all[0:FR, cols_h] = both[0:FR]
        attn_all[R : R + FR, cols_h] = both[FR:]

    def grad_attn():
        acc = jnp.zeros((R, HL * DH), F32)
        for block in range(8):
            acc = acc + dot(cotb[block % 4, block // 4], w[:, block * 384 : (block + 1) * 384], NT)
        acc = acc.astype(BF)
        do2[0:FR, :] = acc[0:FR]
        do_c[...] = acc[FR:R]
        return send(do2.at[own_rows], do2.at[pair_rows], px)

    def weight_grad(h):
        a_t = attn_all[0:R, h * DH : (h + 1) * DH].astype(F32).T.astype(BF)
        for block in range(8):
            p, r = divmod(block, 4)
            g = dot(a_t, cotb[r, p], NN).astype(BF)
            for half in range(2):
                for i in range(3):
                    pw[h, half, r, p, 64 * i : 64 * i + 64, :] = g[
                        64 * half : 64 * half + 64, 128 * i : 128 * i + 128
                    ]

    def coarse_project():
        for block in range(8):
            oc[block % 4, block // 4] = dot(
                attn_all[FR:R, :], w[:, block * 384 : (block + 1) * 384], NN
            ).astype(BF)

    def fine_project():
        for block in range(8):
            of[block % 4, block // 4] = dot(
                attn_all[0:FR, :], w[:, block * 384 : (block + 1) * 384], NN
            ).astype(BF)

    def coarse_backward(h):
        cols_h = slice(h * DH, (h + 1) * DH)
        go = do_c[:, cols_h]
        gof = go.astype(F32)
        delta = jnp.sum(gof * attn_all[FR:R, cols_h].astype(F32), axis=1, keepdims=True)
        gcn[:, cols_h] = (gof * inverse_c[h]).astype(BF)
        dp = dot(go, cv[:, cols_h], NT)
        eb = jnp.concatenate([ecds[h, 0, 0], ecds[h, 1, 0]], axis=1)
        ds = (eb.astype(F32) * ((dp - delta) * (inverse_c[h] * factor))).astype(BF)
        for i in range(2):
            ecds[h, i, 1] = ds[:, HALF * i : HALF * (i + 1)]
        qbuf[core, z, xh, :, cols_h] = dot(ds, ck[:, cols_h], NN).astype(BF)

    def backward(h):
        cols_h = slice(h * DH, (h + 1) * DH)
        go = do2[:, cols_h]
        gof = go.astype(F32)
        attn = jnp.concatenate([attn_all[0:FR, cols_h], attn_all[R : R + FR, cols_h]], axis=0)
        delta = jnp.sum(gof * attn.astype(F32), axis=1, keepdims=True)
        c = inverse[h] * factor
        go_n = (gof * inverse[h]).T.astype(BF)
        q_t = q2[h].astype(F32).T.astype(BF)
        dq = jnp.zeros((2 * FR, DH), F32)
        for j, cols in enumerate(blocks):
            dp = dot(go, value_block(h, j), NT)
            eb = ebuf[h, :, cols]
            ds = (eb.astype(F32) * ((dp - delta) * c)).astype(BF)
            dq = dq + dot(ds, key_block(h, j), NN)
            dk_t = dot(q_t, ds, NN)
            dv_t = dot(go_n, eb, NN)
            if j == 0:
                c_e = jnp.concatenate([ecds[h, xh, 0], ecx[h, 0]], axis=0)
                c_ds = jnp.concatenate([ecds[h, xh, 1], ecx[h, 1]], axis=0)
                c_go = jnp.concatenate([gcn[:, cols_h], gcx[:, cols_h]], axis=0)
                dk = (dk_t.T + dot(c_ds, qc[h], TN)).astype(BF)
                dv = (dv_t.T + dot(c_e, c_go, TN)).astype(BF)
                for r in range(4):
                    for cx in range(2):
                        at = (r * 2 + cx) * CR
                        pa[h, cx, r, 256:288, :] = dk[at : at + CR]
                        pa[h, cx, r, 288:320, :] = dv[at : at + CR]
            else:
                dk_t, dv_t = dk_t.astype(BF), dv_t.astype(BF)
                for r in range(4):
                    pa[h, planes[j - 1], r, 0:128, :] = dk_t[:, 128 * r : 128 * r + 128]
                    pa[h, planes[j - 1], r, 128:256, :] = dv_t[:, 128 * r : 128 * r + 128]
            yield
        fdq_own[h] = dq[0:FR]
        dq_s[:, cols_h] = dq[FR:].astype(BF)

    fdq_own = [None] * HL

    def up(value):
        return value.astype(F32)

    class RingFirst:
        def __init__(self, mine, from_ring, from_pair, rings, ring, pair, ids, pair_id):
            self.mine, self.from_ring, self.from_pair = mine, from_ring, from_pair
            self.rings, self.ring, self.pair, self.ids, self.pair_id = rings, ring, pair, ids, pair_id

        def b(self):
            self.cr = [
                send(self.mine.at[r], self.from_ring.at[i], self.ids[i]) for i, r in enumerate(self.rings)
            ]

        def c(self):
            for copy in self.cr:
                copy.wait_recv()

            def total(p):
                value = up(self.mine[self.ring, p])
                for i in range(3):
                    value = value + up(self.from_ring[i, p])
                return value

            self.mine[self.ring, 1 - self.pair] = total(1 - self.pair).astype(BF)
            self.cx = send(self.mine.at[self.ring, 1 - self.pair], self.from_pair, self.pair_id)
            self.kept = total(self.pair)

        def d(self):
            self.cx.wait_recv()
            return self.kept + up(self.from_pair[...])

    class RingOnly:
        def __init__(self, src, from_sib, from_ring):
            self.src, self.from_sib, self.from_ring = src, from_sib, from_ring

        def a(self):
            self.cs = send(self.src[0], self.from_sib, sib)

        def b(self):
            mine = self.src[1]
            self.cs.wait_recv()
            self.cr = []
            for i, r in enumerate(rings):
                mine[r] = (up(mine[r]) + up(self.from_sib[r])).astype(BF)
                self.cr.append(send(mine.at[r], self.from_ring.at[i], pz[i]))
            self.kept = up(mine[z]) + up(self.from_sib[z])

        def d(self):
            value = self.kept
            for i in range(3):
                self.cr[i].wait_recv()
                value = value + up(self.from_ring[i])
            return value

    class PairFirst:
        def __init__(self, src, from_sib, from_ring, from_pair):
            self.src, self.from_sib, self.from_ring, self.from_pair = src, from_sib, from_ring, from_pair

        def a(self):
            self.cs = send(self.src[0], self.from_sib, sib)

        def b(self):
            mine = self.src[1]
            self.cs.wait_recv()
            p = 1 - xh
            for r in range(4):
                mine[r, p] = (up(mine[r, p]) + up(self.from_sib[r, p])).astype(BF)
            self.cx = send(mine.at[:, p], self.from_pair, px)

        def c(self):
            mine = self.src[1]
            self.cx.wait_recv()

            def total(r):
                return up(mine[r, xh]) + up(self.from_sib[r, xh]) + up(self.from_pair[r])

            self.cr = []
            for i, r in enumerate(rings):
                mine[r, xh] = total(r).astype(BF)
                self.cr.append(send(mine.at[r, xh], self.from_ring.at[i], pz[i]))
            self.kept = total(z)

        def d(self):
            value = self.kept
            for i in range(3):
                self.cr[i].wait_recv()
                value = value + up(self.from_ring[i])
            return value

    sums_a = [RingOnly((pa.at[h, 1 - core], pa.at[h, core]), sa.at[h], az.at[h]) for h in range(HL)]
    sums_w = [
        PairFirst((pw.at[h, 1 - core], pw.at[h, core]), sw.at[h], wz.at[h], wx.at[h]) for h in range(HL)
    ]
    coarse_sum = RingFirst(oc, ocr, ocx, (y2, y1, y3), y, xl, py, pxl)
    fine_sum = RingFirst(of, ofr, ofx, (y2, y1, y3), y, xl, py, pxl)

    out_copies = []

    def store(src, dst):
        copy = pltpu.make_async_copy(src, dst, osem.at[len(out_copies)])
        out_copies.append(copy)
        copy.start()

    lane = lax.broadcasted_iota(jnp.int32, (192, 128), 1)

    def finish_a(h):
        total = sums_a[h].d()
        cols_h = slice(h * DH, (h + 1) * DH)
        fdk[:, cols_h] = total[0:128].T.astype(BF)
        fdv[:, cols_h] = total[128:256].T.astype(BF)
        cdk[:, cols_h] = total[256:288].astype(BF)
        cdv[:, cols_h] = total[288:320].astype(BF)

    def finish_w():
        for h in range(HL):
            total = sums_w[h].d()
            for i in range(3):
                piece = total[64 * i : 64 * i + 64]
                wsend[h, 128 * i : 128 * i + 128, :] = jnp.concatenate([piece, piece], axis=0).T
        other = pl.ds(pl.multiple_of((1 - core) * 192, 64), 192)
        return send(wsend.at[:, other], wrecv, sib)

    def finish_weight(copy):
        copy.wait_recv()
        for h in range(HL):
            mine = wsend[h, pl.ds(pl.multiple_of(core * 192, 64), 192), :]
            wg[:, h * DH : (h + 1) * DH] = jnp.where((lane < 64) == (core == 0), mine, wrecv[h])

    def coarse_done():
        obuf[core, z, xh] = coarse_sum.d().astype(BF)
        out_gather.a()

    def fine_done():
        fout[...] = fine_sum.d().astype(BF)
        store(fout, fout_o)

    def run(steps, events=()):
        todo = list(events)
        for i, _ in enumerate(steps):
            while todo and todo[0][0] <= i:
                todo.pop(0)[1]()
        for _, event in todo:
            event()

    g, A, W = gathers, sums_a, sums_w
    in_ck.wait()
    in_cv.wait()
    for h in range(HL):
        coarse_forward(h)
    gather_a(1)
    in_w.wait()
    coarse_project()
    coarse_sum.b()
    cot_gather.b()
    gather_a(2)
    g[0].d()
    c_scale.wait_recv()
    row_scale[0] = jnp.concatenate([fsc_col, column(scx[...].astype(F32)[0:1])], axis=0)
    c_query.wait_recv()
    g[0].e()
    for i in range(2):
        for r in range(4):
            at = (4 * i + r) * 128
            ksc[:, at : at + 128] = kv[0, planes[i], r, 256:272, :].astype(F32)[0:8]
    x0 = forward(0)
    g[1].d()
    coarse_sum.c()
    g[1].e()
    x1 = forward(1)
    g[2].d()
    cot_gather.d()
    c_do = grad_attn()
    g[2].e()
    x2 = forward(2)
    for h in range(HL):
        coarse_backward(h)
    c_ec = send(ecds.at[:, 1 - xh], ecx, px)
    c_gc = send(gcn, gcx, px)
    combine(0, x0)
    weight_grad(0)
    W[0].a()
    coarse_done()
    dq_gather.a()
    combine(1, x1)
    weight_grad(1)
    W[1].a()
    c_do.wait_recv()
    c_ec.wait_recv()
    c_gc.wait_recv()
    run(backward(0), [(1, A[0].a)])
    W[0].b()
    combine(2, x2)
    weight_grad(2)
    W[2].a()
    A[0].b()
    run(backward(1), [(1, A[1].a)])
    W[1].b()
    fine_project()
    fine_sum.b()
    A[1].b()
    run(backward(2), [(1, A[2].a)])
    W[2].b()
    c_dq = send(dq_s, dq_r, px)
    A[2].b()
    W[0].c()
    out_gather.b()
    dq_gather.b()
    finish_a(0)
    W[1].c()
    out_gather.d()
    dq_gather.d()
    finish_a(1)
    W[2].c()
    fine_sum.c()
    finish_a(2)
    store(fdk, fdk_o)
    store(fdv, fdv_o)
    store(cdk, cdk_o)
    store(cdv, cdv_o)
    c_dq.wait_recv()
    for h in range(HL):
        cols_h = slice(h * DH, (h + 1) * DH)
        fdq[:, cols_h] = (fdq_own[h] + up(dq_r[:, cols_h])).astype(BF)
    store(fdq, fdq_o)
    out_gather.e()
    store(obuf, obuf_o)
    dq_gather.e()
    store(qbuf, qbuf_o)
    c_w = finish_w()
    fine_done()
    finish_weight(c_w)
    store(wg, wg_o)
    for copy in started:
        copy.wait_send()
    for copy in out_copies:
        copy.wait()


def place(fout, fdq, fdk, fdv, cdk, cdv, wg, obuf, qbuf, *rest):
    outs, held, sem_in, sem_out = rest[:9], rest[9:18], rest[18], rest[19]
    loads = [[] for _ in outs]
    for i, src in ((1, fout), (3, cdk), (4, cdv), (5, fdq), (6, fdk), (7, fdv), (8, wg)):
        loads[i].append((src, held[i]))
    for core in range(2):
        for xh in range(2):
            loads[0].append((obuf.at[core, :, xh], held[0].at[xh, :, core]))
            loads[2].append((qbuf.at[core, :, xh], held[2].at[xh, :, core]))
    order = (0, 2, 8, 1, 5, 6, 7, 3, 4)
    copies = {}
    count = 0
    for i in order:
        copies[i] = []
        for src, dst in loads[i]:
            copies[i].append(pltpu.make_async_copy(src, dst, sem_in.at[count]))
            copies[i][-1].start()
            count += 1
    stores = []
    for i in order:
        for copy in copies[i]:
            copy.wait()
        stores.append(pltpu.make_async_copy(held[i], outs[i], sem_out.at[i]))
        stores[-1].start()
    for copy in stores:
        copy.wait()


def on_device(cq, ck, cv, fq, fk, fv, csz, fsz, fpos, w, cc, fc):
    vmem = pl.BlockSpec(memory_space=pltpu.VMEM)
    smem = pl.BlockSpec(memory_space=pltpu.SMEM)
    hbm = pl.BlockSpec(memory_space=pl.ANY)
    shapes = [
        ((128, 384), BF), ((128, 384), BF), ((128, 384), BF), ((128, 384), BF), ((32, 384), BF),
        ((32, 384), BF), ((192, 384), F32), ((2, 4, 2, CR, 384), BF), ((2, 4, 2, CR, 384), BF),
    ]
    v = pltpu.VMEM
    raw = pl.pallas_call(
        kernel,
        out_shape=[jax.ShapeDtypeStruct(s, d) for s, d in shapes],
        in_specs=[hbm] * 6 + [smem] * 2 + [vmem] + [hbm] * 3,
        out_specs=[hbm] * 9,
        scratch_shapes=[
            v((512, 384), BF),
            v((512, 384), BF),
            v((384, 3072), BF),
            v((HL, 2 * FR, DH), BF),
            v((HL, 2 * CR, DH), BF),
            v((HL, 2, 4, KR, DH), BF),
            v((4, 2, R, 384), BF),
            v((16, DH), BF),
            v((8, 1024), F32),
            v((HL, 2 * FR, 1280), F32),
            v((HL, 2 * FR, 1280), BF),
            v((HL, 2, 2, CR, HALF), BF),
            v((HL, 2, CR, HALF), BF),
            v((2 * R, 384), BF),
            v((CR, 384), BF),
            v((CR, 384), BF),
            v((CR, 384), BF),
            v((2 * FR, 384), BF),
            v((HL, 2 * FR, DH), BF),
            v((HL, 2 * FR, DH), BF),
            v((HL, 8, 2 * FR), F32),
            v((HL, 8, 2 * FR), F32),
            v((FR, 384), BF),
            v((FR, 384), BF),
            v((HL, 2, 4, CA, DH), BF),
            v((HL, 2, 4, 2, CW, DH), BF),
            v((HL, 4, CA, DH), BF),
            v((HL, 4, 2, CW, DH), BF),
            v((HL, 3, CA, DH), BF),
            v((HL, 3, CW, DH), BF),
            v((HL, 4, CW, DH), BF),
            v((4, 2, CR, 384), BF),
            v((3, 2, CR, 384), BF),
            v((CR, 384), BF),
            v((4, 2, FR, 384), BF),
            v((3, 2, FR, 384), BF),
            v((FR, 384), BF),
            v((2, 4, 2, CR, 384), BF),
            v((2, 4, 2, CR, 384), BF),
            v((HL, 384, 128), F32),
            v((HL, 192, 128), F32),
            v((128, 384), BF),
            v((128, 384), BF),
            v((128, 384), BF),
            v((128, 384), BF),
            v((32, 384), BF),
            v((32, 384), BF),
            v((192, 384), F32),
            pltpu.SemaphoreType.DMA((96,)),
            pltpu.SemaphoreType.DMA((96,)),
            pltpu.SemaphoreType.DMA((24,)),
            pltpu.SemaphoreType.DMA((9,)),
        ],
        compiler_params=pltpu.CompilerParams(
            collective_id=0, has_side_effects=True, vmem_limit_bytes=56 * 2**20
        ),
        cost_estimate=pl.CostEstimate(flops=7 * 10**9, bytes_accessed=8 * 10**6, transcendentals=1300000),
    )(cq, ck, cv, fq, fk, fv, csz, fsz, fpos.reshape(1, 128), w, cc, fc)
    coarse = ((2, 4, 2, CR, 384), BF)
    fine = ((128, 384), BF)
    small = ((32, 384), BF)
    placed = [coarse, fine, coarse, small, small, fine, fine, fine, ((192, 384), F32)]
    outs = pl.pallas_call(
        place,
        out_shape=[jax.ShapeDtypeStruct(s, d) for s, d in placed],
        in_specs=[hbm] * 9,
        out_specs=[hbm] * 9,
        scratch_shapes=[pltpu.VMEM(s, d) for s, d in placed]
        + [pltpu.SemaphoreType.DMA((15,)), pltpu.SemaphoreType.DMA((9,))],
    )(*raw)
    outs = list(outs)
    outs[0] = outs[0].reshape(512, 384)
    outs[2] = outs[2].reshape(512, 384)
    outs[8] = outs[8].T
    return tuple(outs)


def solution(mesh):
    placed = (
        P(None, "head"), P(None, "head"), P(None, "head"),
        P("ctx", "head"), P("ctx", "head"), P("ctx", "head"),
        P(), P(), P("ctx"), P("head", None), P(None, "head"), P("ctx", "head"),
    )
    return jax.shard_map(
        on_device,
        mesh=mesh,
        in_specs=placed,
        out_specs=(
            P(None, "head"), P("ctx", "head"), P(None, "head"),
            P("ctx", "head"), P("ctx", "head"), P("ctx", "head"),
            P("ctx", "head"), P("ctx", "head"), P("head", "ctx"),
        ),
        check_vma=False,
    )
```

```python
import math

import jax
import jax.numpy as jnp
from jax import lax
from jax.experimental import pallas as pl
from jax.experimental.pallas import tpu as pltpu
from jax.sharding import PartitionSpec as P

DH = 128
HL = 3
FR = 128
CR = 32
R = FR + CR
KR = 272
CA = 320
CW = 192
HALF = 256
NEG = -1e30
BF = jnp.bfloat16
F32 = jnp.float32
MESH = pl.DeviceIdType.MESH
NT = (((1,), (1,)), ((), ()))
TN = (((0,), (0,)), ((), ()))
NN = (((1,), (0,)), ((), ()))


def dot(a, b, dims):
    return lax.dot_general(a, b, dims, preferred_element_type=F32)


def kernel(
    cq, ck_in, cv_in, fq, fk, fv, csz, fsz, fpos, w_in, cc, fc,
    fout_o, fdq_o, fdk_o, fdv_o, cdk_o, cdv_o, wg_o, cbuf_o,
    ck, cv, w, q2, qc, kv, cotb, scx, ksc, tbuf, ebuf, ecds, ecx, attn_all, do_c, gcn, gcx, do2,
    on_s, on_r, st_s, st_r, dq_s, dq_r,
    pa, pw, sa, sw, az, wz, wx,
    oc, ocr, ocx, of, ofr, ofx, cbuf, wsend, wrecv,
    fout, fdq, fdk, fdv, cdk, cdv, wg,
    ssem, rsem, isem, osem,
):
    ctx = lax.axis_index("ctx")
    head = lax.axis_index("head")
    core = ctx % 2
    z = (ctx // 2) % 4
    xh = ctx // 8
    y = head % 4
    xl = head // 4
    z1 = z + 1 - 2 * (z % 2)
    z3 = 3 - z
    z2 = (z + 2) % 4
    y1 = y + 1 - 2 * (y % 2)
    y3 = 3 - y
    y2 = (y + 2) % 4

    def ctx_id(a, b, c):
        return ((a * 4 + b) * 2 + c, head)

    sib = ctx_id(xh, z, 1 - core)
    px = ctx_id(1 - xh, z, core)
    pz1 = ctx_id(xh, z1, core)
    pz3 = ctx_id(xh, z3, core)
    py1 = (ctx, xl * 4 + y1)
    py3 = (ctx, xl * 4 + y3)
    py2 = (ctx, xl * 4 + y2)
    pz2 = ctx_id(xh, z2, core)
    pxl = (ctx, (1 - xl) * 4 + y)
    peers = (px, pz2, pz3, pz1, py2, py3, py1, pxl, sib)

    barrier = pltpu.get_barrier_semaphore()
    for peer in peers:
        pl.semaphore_signal(barrier, inc=1, device_id=peer, device_id_type=MESH)

    loads = [0]

    def load(src, dst):
        copy = pltpu.make_async_copy(src, dst, isem.at[loads[0]])
        loads[0] += 1
        copy.start()
        return copy

    share = pl.ds(pl.multiple_of(ctx * CR, CR), CR)
    pair_share = pl.ds(pl.multiple_of((((1 - xh) * 4 + z) * 2 + core) * CR, CR), CR)
    in_kv = []
    for h in range(HL):
        hs = pl.ds(h * DH, DH)
        in_kv.append((load(fk.at[:, hs], kv.at[h, core, z, pl.ds(0, 128)]), load(fv.at[:, hs], kv.at[h, core, z, pl.ds(128, 128)])))
        if h == 0:
            in_cot = (load(fc, cotb.at[y, xl, pl.ds(0, FR)]), load(cc.at[share], cotb.at[y, xl, pl.ds(FR, CR)]))
    in_q = []
    for h in range(HL):
        hs = pl.ds(h * DH, DH)
        in_q.append((load(fq.at[:, hs], q2.at[h, pl.ds(0, FR)]), load(cq.at[share, hs], qc.at[h, pl.ds(0, CR)]), load(cq.at[pair_share, hs], qc.at[h, pl.ds(CR, CR)])))
    in_ck = load(ck_in, ck)
    in_cv = load(cv_in, cv)
    in_w = load(w_in, w)

    def scale_of(position, sizes, first):
        end = jnp.int32(0)
        total = jnp.zeros(position.shape, jnp.int32) + first
        for s in range(6):
            end = end + sizes[s]
            total = total + (position >= end).astype(jnp.int32)
        return total.astype(F32)

    fsc_row = scale_of(fpos[...], fsz, 6)
    for h in range(HL):
        kv[h, core, z, 256:272, :] = jnp.broadcast_to(fsc_row, (16, 128)).astype(BF)

    count = [0]
    started = []

    def send(src, dst, peer):
        i = count[0]
        count[0] += 1
        copy = pltpu.make_async_remote_copy(
            src_ref=src,
            dst_ref=dst,
            send_sem=ssem.at[i],
            recv_sem=rsem.at[i],
            device_id=peer,
            device_id_type=MESH,
        )
        copy.start()
        started.append(copy)
        return copy

    rings = (z2, z1, z3)
    pz = (pz2, pz1, pz3)
    py = (py2, py1, py3)

    class Gather:
        def __init__(self, at, all_of, ring, pair, ids, pair_id, sibling):
            self.at, self.all_of, self.ring, self.pair = at, all_of, ring, pair
            self.ids, self.pair_id, self.sibling = ids, pair_id, sibling

        def a(self):
            v = self.at(self.ring, self.pair)
            if self.pair_id is not None:
                self.cx = send(v, v, self.pair_id)
            self.waits = [send(v, v, peer) for peer in self.ids]

        def b(self):
            self.cx.wait_recv()
            v = self.at(self.ring, 1 - self.pair)
            self.waits += [send(v, v, peer) for peer in self.ids]

        def d(self):
            for copy in self.waits:
                copy.wait_recv()
            if self.sibling is not None:
                self.cs = send(self.all_of, self.all_of, self.sibling)

        def e(self):
            self.cs.wait_recv()

    gathers = [
        Gather((lambda h: lambda r, p: kv.at[h, core, r])(h), kv.at[h, core], z, None, pz, None, sib)
        for h in range(HL)
    ]
    cot_gather = Gather(lambda r, p: cotb.at[r, p], None, y, xl, py, pxl, None)
    coarse_gather = Gather(lambda r, p: cbuf.at[core, r, p], cbuf.at[core], z, xh, pz, px, sib)

    pl.semaphore_wait(barrier, len(peers))

    def gather_a(h):
        for copy in in_kv[h]:
            copy.wait()
        gathers[h].a()

    for copy in in_cot:
        copy.wait()
    cot_gather.a()
    gather_a(0)
    for copy in in_q[0] + in_q[1] + in_q[2]:
        copy.wait()
    own_rows, pair_rows = pl.ds(0, FR), pl.ds(FR, FR)
    c_scale = send(kv.at[0, core, z, pl.ds(256, 16)], scx, px)
    c_query = send(q2.at[:, own_rows], q2.at[:, pair_rows], px)

    diag = lax.broadcasted_iota(jnp.int32, (128, 128), 0) == lax.broadcasted_iota(
        jnp.int32, (128, 128), 1
    )

    def column(row):
        return jnp.sum(jnp.where(diag, jnp.broadcast_to(row, (128, 128)), 0.0), axis=1, keepdims=True)

    fsc_col = column(fsc_row)
    csc_col = scale_of(lax.broadcasted_iota(jnp.int32, (CR, 1), 0) + ctx * CR, csz, 0)
    csc_row = scale_of(lax.broadcasted_iota(jnp.int32, (1, 512), 1), csz, 0)

    to_log2 = math.log2(math.e) / math.sqrt(DH)
    factor = 1.0 / math.sqrt(DH)
    planes = (1 - core, core)

    blocks = (slice(0, 256), slice(256, 768), slice(768, 1280))
    half_rows = pl.ds(pl.multiple_of(xh * HALF, HALF), HALF)

    def key_block(h, j):
        if j == 0:
            return ck[half_rows, h * DH : (h + 1) * DH]
        return kv[h, planes[j - 1], :, 0:128, :].reshape(512, DH)

    def value_block(h, j):
        if j == 0:
            return cv[half_rows, h * DH : (h + 1) * DH]
        return kv[h, planes[j - 1], :, 128:256, :].reshape(512, DH)

    inverse = [None] * HL
    inverse_c = [None] * HL
    high = [None] * HL
    total = [None] * HL
    row_scale = [None]

    def coarse_forward(h):
        cols_h = slice(h * DH, (h + 1) * DH)
        s = dot(qc[h, 0:CR, :], ck[:, cols_h], NT) * to_log2
        s = jnp.where(csc_row <= csc_col, s, NEG)
        e = jnp.exp2(s - jnp.max(s, axis=1, keepdims=True))
        inverse_c[h] = 1.0 / jnp.sum(e, axis=1, keepdims=True)
        eb = e.astype(BF)
        for i in range(2):
            ecds[h, i, 0] = eb[:, HALF * i : HALF * (i + 1)]
        acc = dot(eb, cv[:, cols_h], NN)
        attn_all[FR:R, cols_h] = (acc * inverse_c[h]).astype(BF)

    def forward(h):
        m = None
        for j, cols in enumerate(blocks):
            s = dot(q2[h], key_block(h, j), NT) * to_log2
            if j > 0:
                s = jnp.where(ksc[0:1, cols.start - 256 : cols.stop - 256] <= row_scale[0], s, NEG)
            tbuf[h, :, cols] = s
            top = jnp.max(s, axis=1, keepdims=True)
            m = top if m is None else jnp.maximum(m, top)
        l = jnp.zeros((2 * FR, 1), F32)
        acc = jnp.zeros((2 * FR, DH), F32)
        for j, cols in enumerate(blocks):
            e = jnp.exp2(tbuf[h, :, cols] - m)
            l = l + jnp.sum(e, axis=1, keepdims=True)
            eb = e.astype(BF)
            ebuf[h, :, cols] = eb
            acc = acc + dot(eb, value_block(h, j), NN)
        high[h], total[h] = m, l
        on_s[h] = (acc * (1.0 / l)).astype(BF)
        lane2 = lax.broadcasted_iota(jnp.int32, (2 * FR, 128), 1)
        st_s[h] = jnp.where(lane2 == 0, m, l).T[0:8]
        return send(on_s.at[h], on_r.at[h], px), send(st_s.at[h], st_r.at[h], px)

    def swapped(v):
        return jnp.concatenate([v[FR:], v[:FR]], axis=0)

    def combine(h, copies):
        for copy in copies:
            copy.wait_recv()
        st = swapped(jnp.concatenate([st_r[h]] * 16, axis=0).T)
        m2, l2 = st[:, 0:1], st[:, 1:2]
        m1, l1 = high[h], total[h]
        m = jnp.maximum(m1, m2)
        f1 = jnp.exp2(m1 - m)
        w1, w2 = l1 * f1, l2 * jnp.exp2(m2 - m)
        rl = 1.0 / (w1 + w2)
        inverse[h] = f1 * rl
        both = on_s[h].astype(F32) * (w1 * rl) + swapped(on_r[h].astype(F32)) * (w2 * rl)
        both = both.astype(BF)
        cols_h = slice(h * DH, (h + 1) * DH)
        attn_all[0:FR, cols_h] = both[0:FR]
        attn_all[R : R + FR, cols_h] = both[FR:]

    def grad_attn():
        acc = jnp.zeros((R, HL * DH), F32)
        for block in range(8):
            acc = acc + dot(cotb[block % 4, block // 4], w[:, block * 384 : (block + 1) * 384], NT)
        acc = acc.astype(BF)
        do2[0:FR, :] = acc[0:FR]
        do_c[...] = acc[FR:R]
        return send(do2.at[own_rows], do2.at[pair_rows], px)

    def weight_grad(h):
        a_t = attn_all[0:R, h * DH : (h + 1) * DH].astype(F32).T.astype(BF)
        for block in range(8):
            p, r = divmod(block, 4)
            g = dot(a_t, cotb[r, p], NN).astype(BF)
            for half in range(2):
                for i in range(3):
                    pw[h, half, r, p, 64 * i : 64 * i + 64, :] = g[
                        64 * half : 64 * half + 64, 128 * i : 128 * i + 128
                    ]

    def coarse_project():
        for block in range(8):
            oc[block % 4, block // 4] = dot(
                attn_all[FR:R, :], w[:, block * 384 : (block + 1) * 384], NN
            ).astype(BF)

    def fine_project():
        for block in range(8):
            of[block % 4, block // 4] = dot(
                attn_all[0:FR, :], w[:, block * 384 : (block + 1) * 384], NN
            ).astype(BF)

    def coarse_backward(h):
        cols_h = slice(h * DH, (h + 1) * DH)
        go = do_c[:, cols_h]
        gof = go.astype(F32)
        delta = jnp.sum(gof * attn_all[FR:R, cols_h].astype(F32), axis=1, keepdims=True)
        gcn[:, cols_h] = (gof * inverse_c[h]).astype(BF)
        dp = dot(go, cv[:, cols_h], NT)
        eb = jnp.concatenate([ecds[h, 0, 0], ecds[h, 1, 0]], axis=1)
        ds = (eb.astype(F32) * ((dp - delta) * (inverse_c[h] * factor))).astype(BF)
        for i in range(2):
            ecds[h, i, 1] = ds[:, HALF * i : HALF * (i + 1)]
        cbuf[core, z, xh, CR : 2 * CR, cols_h] = dot(ds, ck[:, cols_h], NN).astype(BF)

    def backward(h):
        cols_h = slice(h * DH, (h + 1) * DH)
        go = do2[:, cols_h]
        gof = go.astype(F32)
        attn = jnp.concatenate([attn_all[0:FR, cols_h], attn_all[R : R + FR, cols_h]], axis=0)
        delta = jnp.sum(gof * attn.astype(F32), axis=1, keepdims=True)
        c = inverse[h] * factor
        go_n = (gof * inverse[h]).T.astype(BF)
        q_t = q2[h].astype(F32).T.astype(BF)
        dq = jnp.zeros((2 * FR, DH), F32)
        for j, cols in enumerate(blocks):
            dp = dot(go, value_block(h, j), NT)
            eb = ebuf[h, :, cols]
            ds = (eb.astype(F32) * ((dp - delta) * c)).astype(BF)
            dq = dq + dot(ds, key_block(h, j), NN)
            dk_t = dot(q_t, ds, NN)
            dv_t = dot(go_n, eb, NN)
            if j == 0:
                c_e = jnp.concatenate([ecds[h, xh, 0], ecx[h, 0]], axis=0)
                c_ds = jnp.concatenate([ecds[h, xh, 1], ecx[h, 1]], axis=0)
                c_go = jnp.concatenate([gcn[:, cols_h], gcx[:, cols_h]], axis=0)
                dk = (dk_t.T + dot(c_ds, qc[h], TN)).astype(BF)
                dv = (dv_t.T + dot(c_e, c_go, TN)).astype(BF)
                for r in range(4):
                    for cx in range(2):
                        at = (r * 2 + cx) * CR
                        pa[h, cx, r, 256:288, :] = dk[at : at + CR]
                        pa[h, cx, r, 288:320, :] = dv[at : at + CR]
            else:
                dk_t, dv_t = dk_t.astype(BF), dv_t.astype(BF)
                for r in range(4):
                    pa[h, planes[j - 1], r, 0:128, :] = dk_t[:, 128 * r : 128 * r + 128]
                    pa[h, planes[j - 1], r, 128:256, :] = dv_t[:, 128 * r : 128 * r + 128]
            yield
        fdq_own[h] = dq[0:FR]
        dq_s[:, cols_h] = dq[FR:].astype(BF)

    fdq_own = [None] * HL

    def up(value):
        return value.astype(F32)

    class RingFirst:
        def __init__(self, mine, from_ring, from_pair, rings, ring, pair, ids, pair_id):
            self.mine, self.from_ring, self.from_pair = mine, from_ring, from_pair
            self.rings, self.ring, self.pair, self.ids, self.pair_id = rings, ring, pair, ids, pair_id

        def b(self):
            self.cr = [
                send(self.mine.at[r], self.from_ring.at[i], self.ids[i]) for i, r in enumerate(self.rings)
            ]

        def c(self):
            for copy in self.cr:
                copy.wait_recv()

            def total(p):
                value = up(self.mine[self.ring, p])
                for i in range(3):
                    value = value + up(self.from_ring[i, p])
                return value

            self.mine[self.ring, 1 - self.pair] = total(1 - self.pair).astype(BF)
            self.cx = send(self.mine.at[self.ring, 1 - self.pair], self.from_pair, self.pair_id)
            self.kept = total(self.pair)

        def d(self):
            self.cx.wait_recv()
            return self.kept + up(self.from_pair[...])

    class RingOnly:
        def __init__(self, src, from_sib, from_ring):
            self.src, self.from_sib, self.from_ring = src, from_sib, from_ring

        def a(self):
            self.cs = send(self.src[0], self.from_sib, sib)

        def b(self):
            mine = self.src[1]
            self.cs.wait_recv()
            self.cr = []
            for i, r in enumerate(rings):
                mine[r] = (up(mine[r]) + up(self.from_sib[r])).astype(BF)
                self.cr.append(send(mine.at[r], self.from_ring.at[i], pz[i]))
            self.kept = up(mine[z]) + up(self.from_sib[z])

        def d(self):
            value = self.kept
            for i in range(3):
                self.cr[i].wait_recv()
                value = value + up(self.from_ring[i])
            return value

    class PairFirst:
        def __init__(self, src, from_sib, from_ring, from_pair):
            self.src, self.from_sib, self.from_ring, self.from_pair = src, from_sib, from_ring, from_pair

        def a(self):
            self.cs = send(self.src[0], self.from_sib, sib)

        def b(self):
            mine = self.src[1]
            self.cs.wait_recv()
            p = 1 - xh
            for r in range(4):
                mine[r, p] = (up(mine[r, p]) + up(self.from_sib[r, p])).astype(BF)
            self.cx = send(mine.at[:, p], self.from_pair, px)

        def c(self):
            mine = self.src[1]
            self.cx.wait_recv()

            def total(r):
                return up(mine[r, xh]) + up(self.from_sib[r, xh]) + up(self.from_pair[r])

            self.cr = []
            for i, r in enumerate(rings):
                mine[r, xh] = total(r).astype(BF)
                self.cr.append(send(mine.at[r, xh], self.from_ring.at[i], pz[i]))
            self.kept = total(z)

        def d(self):
            value = self.kept
            for i in range(3):
                self.cr[i].wait_recv()
                value = value + up(self.from_ring[i])
            return value

    class RingPair:
        def __init__(self, src, from_sib, from_ring, from_pair):
            self.src, self.from_sib, self.from_ring, self.from_pair = src, from_sib, from_ring, from_pair

        def a(self):
            self.cs = send(self.src[0], self.from_sib, sib)

        def b(self):
            mine = self.src[1]
            self.cs.wait_recv()
            self.cr = []
            for i, r in enumerate(rings):
                mine[r] = (up(mine[r]) + up(self.from_sib[r])).astype(BF)
                self.cr.append(send(mine.at[r], self.from_ring.at[i], pz[i]))

        def c(self):
            mine = self.src[1]
            for copy in self.cr:
                copy.wait_recv()

            def total(p):
                value = up(mine[z, p]) + up(self.from_sib[z, p])
                for i in range(3):
                    value = value + up(self.from_ring[i, p])
                return value

            mine[z, 1 - xh] = total(1 - xh).astype(BF)
            self.cx = send(mine.at[z, 1 - xh], self.from_pair, px)
            self.kept = total(xh)

        def d(self):
            self.cx.wait_recv()
            return self.kept + up(self.from_pair[...])

    sums_a = [RingOnly((pa.at[h, 1 - core], pa.at[h, core]), sa.at[h], az.at[h]) for h in range(HL)]
    sums_w = [
        RingPair((pw.at[h, 1 - core], pw.at[h, core]), sw.at[h], wz.at[h], wx.at[h, 0])
        if h < 2
        else PairFirst((pw.at[h, 1 - core], pw.at[h, core]), sw.at[h], wz.at[h, :, 0], wx.at[h])
        for h in range(HL)
    ]
    coarse_sum = RingFirst(oc, ocr, ocx, (y2, y1, y3), y, xl, py, pxl)
    fine_sum = RingFirst(of, ofr, ofx, (y2, y1, y3), y, xl, py, pxl)

    out_copies = []

    def store(src, dst):
        copy = pltpu.make_async_copy(src, dst, osem.at[len(out_copies)])
        out_copies.append(copy)
        copy.start()

    lane = lax.broadcasted_iota(jnp.int32, (192, 128), 1)

    def finish_a(h):
        total = sums_a[h].d()
        cols_h = slice(h * DH, (h + 1) * DH)
        fdk[:, cols_h] = total[0:128].T.astype(BF)
        fdv[:, cols_h] = total[128:256].T.astype(BF)
        cdk[:, cols_h] = total[256:288].astype(BF)
        cdv[:, cols_h] = total[288:320].astype(BF)

    def finish_w(h):
        total = sums_w[h].d()
        for i in range(3):
            piece = total[64 * i : 64 * i + 64]
            wsend[h, 128 * i : 128 * i + 128, :] = jnp.concatenate([piece, piece], axis=0).T
        other = pl.ds(pl.multiple_of((1 - core) * 192, 64), 192)
        return send(wsend.at[h, other], wrecv.at[h], sib)

    def finish_weight(h, copy):
        copy.wait_recv()
        mine = wsend[h, pl.ds(pl.multiple_of(core * 192, 64), 192), :]
        wg[:, h * DH : (h + 1) * DH] = jnp.where((lane < 64) == (core == 0), mine, wrecv[h])

    def coarse_done():
        cbuf[core, z, xh, 0:CR, :] = coarse_sum.d().astype(BF)
        coarse_gather.a()

    def fine_done():
        fout[...] = fine_sum.d().astype(BF)
        store(fout, fout_o)

    def run(steps, events=()):
        todo = list(events)
        for i, _ in enumerate(steps):
            while todo and todo[0][0] <= i:
                todo.pop(0)[1]()
        for _, event in todo:
            event()

    g, A, W = gathers, sums_a, sums_w
    in_ck.wait()
    in_cv.wait()
    for h in range(HL):
        coarse_forward(h)
    gather_a(1)
    cot_gather.b()
    gather_a(2)
    in_w.wait()
    coarse_project()
    coarse_sum.b()
    g[0].d()
    c_scale.wait_recv()
    row_scale[0] = jnp.concatenate([fsc_col, column(scx[...].astype(F32)[0:1])], axis=0)
    c_query.wait_recv()
    g[0].e()
    for i in range(2):
        for r in range(4):
            at = (4 * i + r) * 128
            ksc[:, at : at + 128] = kv[0, planes[i], r, 256:272, :].astype(F32)[0:8]
    x0 = forward(0)
    g[1].d()
    g[1].e()
    x1 = forward(1)
    g[2].d()
    g[2].e()
    x2 = forward(2)
    cot_gather.d()
    c_do = grad_attn()
    for h in range(HL):
        coarse_backward(h)
    c_ec = send(ecds.at[:, 1 - xh], ecx, px)
    c_gc = send(gcn, gcx, px)
    combine(0, x0)
    weight_grad(0)
    W[0].a()
    combine(1, x1)
    weight_grad(1)
    W[1].a()
    W[0].b()
    coarse_sum.c()
    c_do.wait_recv()
    c_ec.wait_recv()
    c_gc.wait_recv()
    coarse_done()
    run(backward(0), [(1, A[0].a)])
    W[1].b()
    combine(2, x2)
    weight_grad(2)
    W[2].a()
    A[0].b()
    run(backward(1), [(1, A[1].a)])
    W[2].b()
    coarse_gather.b()
    fine_project()
    fine_sum.b()
    A[1].b()
    run(backward(2), [(1, A[2].a)])
    c_dq = send(dq_s, dq_r, px)
    W[0].c()
    A[2].b()
    W[1].c()
    finish_a(0)
    W[2].c()
    c_w0 = finish_w(0)
    finish_a(1)
    c_w1 = finish_w(1)
    coarse_gather.d()
    fine_sum.c()
    c_dq.wait_recv()
    for h in range(HL):
        cols_h = slice(h * DH, (h + 1) * DH)
        fdq[:, cols_h] = (fdq_own[h] + up(dq_r[:, cols_h])).astype(BF)
    store(fdq, fdq_o)
    finish_a(2)
    store(fdk, fdk_o)
    store(fdv, fdv_o)
    store(cdk, cdk_o)
    store(cdv, cdv_o)
    c_w2 = finish_w(2)
    finish_weight(0, c_w0)
    finish_weight(1, c_w1)
    coarse_gather.e()
    store(cbuf, cbuf_o)
    fine_done()
    finish_weight(2, c_w2)
    store(wg, wg_o)
    for copy in started:
        copy.wait_send()
    for copy in out_copies:
        copy.wait()


def place(fout, fdq, fdk, fdv, cdk, cdv, wg, cbuf, *rest):
    outs, held, sem_in, sem_out = rest[:9], rest[9:18], rest[18], rest[19]
    loads = [[] for _ in outs]
    for i, src in ((1, fout), (3, cdk), (4, cdv), (5, fdq), (6, fdk), (7, fdv), (8, wg)):
        loads[i].append((src, held[i]))
    for core in range(2):
        for xh in range(2):
            loads[0].append((cbuf.at[core, :, xh, pl.ds(0, CR)], held[0].at[xh, :, core]))
            loads[2].append((cbuf.at[core, :, xh, pl.ds(CR, CR)], held[2].at[xh, :, core]))
    order = (0, 2, 8, 1, 5, 6, 7, 3, 4)
    copies = {}
    count = 0
    for i in order:
        copies[i] = []
        for src, dst in loads[i]:
            copies[i].append(pltpu.make_async_copy(src, dst, sem_in.at[count]))
            copies[i][-1].start()
            count += 1
    stores = []
    for i in order:
        for copy in copies[i]:
            copy.wait()
        stores.append(pltpu.make_async_copy(held[i], outs[i], sem_out.at[i]))
        stores[-1].start()
    for copy in stores:
        copy.wait()


def on_device(cq, ck, cv, fq, fk, fv, csz, fsz, fpos, w, cc, fc):
    vmem = pl.BlockSpec(memory_space=pltpu.VMEM)
    smem = pl.BlockSpec(memory_space=pltpu.SMEM)
    hbm = pl.BlockSpec(memory_space=pl.ANY)
    shapes = [
        ((128, 384), BF), ((128, 384), BF), ((128, 384), BF), ((128, 384), BF), ((32, 384), BF),
        ((32, 384), BF), ((192, 384), F32), ((2, 4, 2, 2 * CR, 384), BF),
    ]
    v = pltpu.VMEM
    raw = pl.pallas_call(
        kernel,
        out_shape=[jax.ShapeDtypeStruct(s, d) for s, d in shapes],
        in_specs=[hbm] * 6 + [smem] * 2 + [vmem] + [hbm] * 3,
        out_specs=[hbm] * 8,
        scratch_shapes=[
            v((512, 384), BF),
            v((512, 384), BF),
            v((384, 3072), BF),
            v((HL, 2 * FR, DH), BF),
            v((HL, 2 * CR, DH), BF),
            v((HL, 2, 4, KR, DH), BF),
            v((4, 2, R, 384), BF),
            v((16, DH), BF),
            v((8, 1024), F32),
            v((HL, 2 * FR, 1280), F32),
            v((HL, 2 * FR, 1280), BF),
            v((HL, 2, 2, CR, HALF), BF),
            v((HL, 2, CR, HALF), BF),
            v((2 * R, 384), BF),
            v((CR, 384), BF),
            v((CR, 384), BF),
            v((CR, 384), BF),
            v((2 * FR, 384), BF),
            v((HL, 2 * FR, DH), BF),
            v((HL, 2 * FR, DH), BF),
            v((HL, 8, 2 * FR), F32),
            v((HL, 8, 2 * FR), F32),
            v((FR, 384), BF),
            v((FR, 384), BF),
            v((HL, 2, 4, CA, DH), BF),
            v((HL, 2, 4, 2, CW, DH), BF),
            v((HL, 4, CA, DH), BF),
            v((HL, 4, 2, CW, DH), BF),
            v((HL, 3, CA, DH), BF),
            v((HL, 3, 2, CW, DH), BF),
            v((HL, 4, CW, DH), BF),
            v((4, 2, CR, 384), BF),
            v((3, 2, CR, 384), BF),
            v((CR, 384), BF),
            v((4, 2, FR, 384), BF),
            v((3, 2, FR, 384), BF),
            v((FR, 384), BF),
            v((2, 4, 2, 2 * CR, 384), BF),
            v((HL, 384, 128), F32),
            v((HL, 192, 128), F32),
            v((128, 384), BF),
            v((128, 384), BF),
            v((128, 384), BF),
            v((128, 384), BF),
            v((32, 384), BF),
            v((32, 384), BF),
            v((192, 384), F32),
            pltpu.SemaphoreType.DMA((96,)),
            pltpu.SemaphoreType.DMA((96,)),
            pltpu.SemaphoreType.DMA((24,)),
            pltpu.SemaphoreType.DMA((9,)),
        ],
        compiler_params=pltpu.CompilerParams(
            collective_id=0, has_side_effects=True, vmem_limit_bytes=56 * 2**20
        ),
        cost_estimate=pl.CostEstimate(flops=7 * 10**9, bytes_accessed=8 * 10**6, transcendentals=1300000),
    )(cq, ck, cv, fq, fk, fv, csz, fsz, fpos.reshape(1, 128), w, cc, fc)
    coarse = ((2, 4, 2, CR, 384), BF)
    fine = ((128, 384), BF)
    small = ((32, 384), BF)
    placed = [coarse, fine, coarse, small, small, fine, fine, fine, ((192, 384), F32)]
    outs = pl.pallas_call(
        place,
        out_shape=[jax.ShapeDtypeStruct(s, d) for s, d in placed],
        in_specs=[hbm] * 8,
        out_specs=[hbm] * 9,
        scratch_shapes=[pltpu.VMEM(s, d) for s, d in placed]
        + [pltpu.SemaphoreType.DMA((15,)), pltpu.SemaphoreType.DMA((9,))],
    )(*raw)
    outs = list(outs)
    outs[0] = outs[0].reshape(512, 384)
    outs[2] = outs[2].reshape(512, 384)
    outs[8] = outs[8].T
    return tuple(outs)


def solution(mesh):
    placed = (
        P(None, "head"), P(None, "head"), P(None, "head"),
        P("ctx", "head"), P("ctx", "head"), P("ctx", "head"),
        P(), P(), P("ctx"), P("head", None), P(None, "head"), P("ctx", "head"),
    )
    return jax.shard_map(
        on_device,
        mesh=mesh,
        in_specs=placed,
        out_specs=(
            P(None, "head"), P("ctx", "head"), P(None, "head"),
            P("ctx", "head"), P("ctx", "head"), P("ctx", "head"),
            P("ctx", "head"), P("ctx", "head"), P("head", "ctx"),
        ),
        check_vma=False,
    )
```

```python
import math

import jax
import jax.numpy as jnp
from jax import lax
from jax.experimental import pallas as pl
from jax.experimental.pallas import tpu as pltpu
from jax.sharding import PartitionSpec as P

DH = 128
HL = 3
FR = 128
CR = 32
R = FR + CR
KR = 272
CA = 320
CW = 192
HALF = 256
NEG = -1e30
BF = jnp.bfloat16
F32 = jnp.float32
MESH = pl.DeviceIdType.MESH
NT = (((1,), (1,)), ((), ()))
TN = (((0,), (0,)), ((), ()))
NN = (((1,), (0,)), ((), ()))


def dot(a, b, dims):
    return lax.dot_general(a, b, dims, preferred_element_type=F32)


def kernel(
    cq, ck_in, cv_in, fq, fk, fv, csz, fsz, fpos, w_in, cc, fc,
    fout_o, fdq_o, fdk_o, fdv_o, cdk_o, cdv_o, wg_o, cbuf_o,
    ck, cv, w, q2, qc, kv, cotb, scx, ksc, tbuf, ebuf, ecds, ecx, attn_all, do_c, gcn, gcx, do2,
    on_s, on_r, st_s, st_r, dq_s, dq_r,
    pa, pw, sa, sw, az, wz, wx,
    oc, ocr, ocx, of, ofr, ofx, cbuf, wsend, wrecv,
    fout, fdq, fdk, fdv, cdk, cdv, wg,
    ssem, rsem, isem, osem,
):
    ctx = lax.axis_index("ctx")
    head = lax.axis_index("head")
    core = ctx % 2
    z = (ctx // 2) % 4
    xh = ctx // 8
    y = head % 4
    xl = head // 4
    z1 = z + 1 - 2 * (z % 2)
    z3 = 3 - z
    z2 = (z + 2) % 4
    y1 = y + 1 - 2 * (y % 2)
    y3 = 3 - y
    y2 = (y + 2) % 4

    def ctx_id(a, b, c):
        return ((a * 4 + b) * 2 + c, head)

    sib = ctx_id(xh, z, 1 - core)
    px = ctx_id(1 - xh, z, core)
    pz1 = ctx_id(xh, z1, core)
    pz3 = ctx_id(xh, z3, core)
    py1 = (ctx, xl * 4 + y1)
    py3 = (ctx, xl * 4 + y3)
    py2 = (ctx, xl * 4 + y2)
    pz2 = ctx_id(xh, z2, core)
    pxl = (ctx, (1 - xl) * 4 + y)
    peers = (px, pz2, pz3, pz1, py2, py3, py1, pxl, sib)

    barrier = pltpu.get_barrier_semaphore()
    for peer in peers:
        pl.semaphore_signal(barrier, inc=1, device_id=peer, device_id_type=MESH)

    loads = [0]

    def load(src, dst):
        copy = pltpu.make_async_copy(src, dst, isem.at[loads[0]])
        loads[0] += 1
        copy.start()
        return copy

    share = pl.ds(pl.multiple_of(ctx * CR, CR), CR)
    pair_share = pl.ds(pl.multiple_of((((1 - xh) * 4 + z) * 2 + core) * CR, CR), CR)
    in_kv = []
    for h in range(HL):
        hs = pl.ds(h * DH, DH)
        in_kv.append((load(fk.at[:, hs], kv.at[h, core, z, pl.ds(0, 128)]), load(fv.at[:, hs], kv.at[h, core, z, pl.ds(128, 128)])))
        if h == 0:
            in_cot = (load(fc, cotb.at[y, xl, pl.ds(0, FR)]), load(cc.at[share], cotb.at[y, xl, pl.ds(FR, CR)]))
    in_q = []
    for h in range(HL):
        hs = pl.ds(h * DH, DH)
        in_q.append((load(fq.at[:, hs], q2.at[h, pl.ds(0, FR)]), load(cq.at[share, hs], qc.at[h, pl.ds(0, CR)]), load(cq.at[pair_share, hs], qc.at[h, pl.ds(CR, CR)])))
    in_ck = load(ck_in, ck)
    in_cv = load(cv_in, cv)
    in_w = load(w_in, w)

    def scale_of(position, sizes, first):
        end = jnp.int32(0)
        total = jnp.zeros(position.shape, jnp.int32) + first
        for s in range(6):
            end = end + sizes[s]
            total = total + (position >= end).astype(jnp.int32)
        return total.astype(F32)

    fsc_row = scale_of(fpos[...], fsz, 6)
    for h in range(HL):
        kv[h, core, z, 256:272, :] = jnp.broadcast_to(fsc_row, (16, 128)).astype(BF)

    count = [0]
    started = []

    def send(src, dst, peer):
        i = count[0]
        count[0] += 1
        copy = pltpu.make_async_remote_copy(
            src_ref=src,
            dst_ref=dst,
            send_sem=ssem.at[i],
            recv_sem=rsem.at[i],
            device_id=peer,
            device_id_type=MESH,
        )
        copy.start()
        started.append(copy)
        return copy

    rings = (z2, z1, z3)
    pz = (pz2, pz1, pz3)
    py = (py2, py1, py3)

    class Gather:
        def __init__(self, at, all_of, ring, pair, ids, pair_id, sibling):
            self.at, self.all_of, self.ring, self.pair = at, all_of, ring, pair
            self.ids, self.pair_id, self.sibling = ids, pair_id, sibling

        def a(self):
            v = self.at(self.ring, self.pair)
            if self.pair_id is not None:
                self.cx = send(v, v, self.pair_id)
            self.waits = [send(v, v, peer) for peer in self.ids]

        def b(self):
            self.cx.wait_recv()
            v = self.at(self.ring, 1 - self.pair)
            self.waits += [send(v, v, peer) for peer in self.ids]

        def d(self):
            for copy in self.waits:
                copy.wait_recv()
            if self.sibling is not None:
                self.cs = send(self.all_of, self.all_of, self.sibling)

        def e(self):
            self.cs.wait_recv()

    gathers = [
        Gather((lambda h: lambda r, p: kv.at[h, core, r])(h), kv.at[h, core], z, None, pz, None, sib)
        for h in range(HL)
    ]
    cot_gather = Gather(lambda r, p: cotb.at[r, p], None, y, xl, py, pxl, None)
    coarse_gather = Gather(lambda r, p: cbuf.at[core, r, p], cbuf.at[core], z, xh, pz, px, sib)

    pl.semaphore_wait(barrier, len(peers))

    def gather_a(h):
        for copy in in_kv[h]:
            copy.wait()
        gathers[h].a()

    for copy in in_cot:
        copy.wait()
    cot_gather.a()
    gather_a(0)
    for copy in in_q[0] + in_q[1] + in_q[2]:
        copy.wait()
    own_rows, pair_rows = pl.ds(0, FR), pl.ds(FR, FR)
    c_scale = send(kv.at[0, core, z, pl.ds(256, 16)], scx, px)
    c_query = send(q2.at[:, own_rows], q2.at[:, pair_rows], px)

    diag = lax.broadcasted_iota(jnp.int32, (128, 128), 0) == lax.broadcasted_iota(
        jnp.int32, (128, 128), 1
    )

    def column(row):
        return jnp.sum(jnp.where(diag, jnp.broadcast_to(row, (128, 128)), 0.0), axis=1, keepdims=True)

    fsc_col = column(fsc_row)
    csc_col = scale_of(lax.broadcasted_iota(jnp.int32, (CR, 1), 0) + ctx * CR, csz, 0)
    csc_row = scale_of(lax.broadcasted_iota(jnp.int32, (1, 512), 1), csz, 0)

    to_log2 = math.log2(math.e) / math.sqrt(DH)
    factor = 1.0 / math.sqrt(DH)
    planes = (1 - core, core)

    blocks = (slice(0, 256), slice(256, 768), slice(768, 1280))
    half_rows = pl.ds(pl.multiple_of(xh * HALF, HALF), HALF)

    def key_block(h, j):
        if j == 0:
            return ck[half_rows, h * DH : (h + 1) * DH]
        return kv[h, planes[j - 1], :, 0:128, :].reshape(512, DH)

    def value_block(h, j):
        if j == 0:
            return cv[half_rows, h * DH : (h + 1) * DH]
        return kv[h, planes[j - 1], :, 128:256, :].reshape(512, DH)

    inverse = [None] * HL
    inverse_c = [None] * HL
    high = [None] * HL
    total = [None] * HL
    row_scale = [None]

    def coarse_forward(h):
        cols_h = slice(h * DH, (h + 1) * DH)
        s = dot(qc[h, 0:CR, :], ck[:, cols_h], NT) * to_log2
        s = jnp.where(csc_row <= csc_col, s, NEG)
        e = jnp.exp2(s - jnp.max(s, axis=1, keepdims=True))
        inverse_c[h] = 1.0 / jnp.sum(e, axis=1, keepdims=True)
        eb = e.astype(BF)
        for i in range(2):
            ecds[h, i, 0] = eb[:, HALF * i : HALF * (i + 1)]
        acc = dot(eb, cv[:, cols_h], NN)
        attn_all[FR:R, cols_h] = (acc * inverse_c[h]).astype(BF)

    def forward(h):
        m = None
        for j, cols in enumerate(blocks):
            s = dot(q2[h], key_block(h, j), NT) * to_log2
            if j > 0:
                s = jnp.where(ksc[0:1, cols.start - 256 : cols.stop - 256] <= row_scale[0], s, NEG)
            tbuf[h, :, cols] = s
            top = jnp.max(s, axis=1, keepdims=True)
            m = top if m is None else jnp.maximum(m, top)
        l = jnp.zeros((2 * FR, 1), F32)
        acc = jnp.zeros((2 * FR, DH), F32)
        for j, cols in enumerate(blocks):
            e = jnp.exp2(tbuf[h, :, cols] - m)
            l = l + jnp.sum(e, axis=1, keepdims=True)
            eb = e.astype(BF)
            ebuf[h, :, cols] = eb
            acc = acc + dot(eb, value_block(h, j), NN)
        high[h], total[h] = m, l
        on_s[h] = (acc * (1.0 / l)).astype(BF)
        lane2 = lax.broadcasted_iota(jnp.int32, (2 * FR, 128), 1)
        st_s[h] = jnp.where(lane2 == 0, m, l).T[0:8]
        return send(on_s.at[h], on_r.at[h], px), send(st_s.at[h], st_r.at[h], px)

    def swapped(v):
        return jnp.concatenate([v[FR:], v[:FR]], axis=0)

    def combine(h, copies):
        for copy in copies:
            copy.wait_recv()
        st = swapped(jnp.concatenate([st_r[h]] * 16, axis=0).T)
        m2, l2 = st[:, 0:1], st[:, 1:2]
        m1, l1 = high[h], total[h]
        m = jnp.maximum(m1, m2)
        f1 = jnp.exp2(m1 - m)
        w1, w2 = l1 * f1, l2 * jnp.exp2(m2 - m)
        rl = 1.0 / (w1 + w2)
        inverse[h] = f1 * rl
        both = on_s[h].astype(F32) * (w1 * rl) + swapped(on_r[h].astype(F32)) * (w2 * rl)
        both = both.astype(BF)
        cols_h = slice(h * DH, (h + 1) * DH)
        attn_all[0:FR, cols_h] = both[0:FR]
        attn_all[R : R + FR, cols_h] = both[FR:]

    def grad_attn(h):
        cols_h = slice(h * DH, (h + 1) * DH)
        acc = jnp.zeros((R, DH), F32)
        for block in range(8):
            acc = acc + dot(cotb[block % 4, block // 4], w[cols_h, block * 384 : (block + 1) * 384], NT)
        acc = acc.astype(BF)
        do2[0:FR, cols_h] = acc[0:FR]
        do_c[:, cols_h] = acc[FR:R]
        hs = pl.ds(h * DH, DH)
        return send(do2.at[own_rows, hs], do2.at[pair_rows, hs], px)

    def weight_grad(h):
        a_t = attn_all[0:R, h * DH : (h + 1) * DH].astype(F32).T.astype(BF)
        for block in range(8):
            p, r = divmod(block, 4)
            g = dot(a_t, cotb[r, p], NN).astype(BF)
            for half in range(2):
                for i in range(3):
                    pw[h, half, r, p, 64 * i : 64 * i + 64, :] = g[
                        64 * half : 64 * half + 64, 128 * i : 128 * i + 128
                    ]

    def coarse_project():
        for block in range(8):
            oc[block % 4, block // 4] = dot(
                attn_all[FR:R, :], w[:, block * 384 : (block + 1) * 384], NN
            ).astype(BF)

    def fine_project():
        for block in range(8):
            of[block % 4, block // 4] = dot(
                attn_all[0:FR, :], w[:, block * 384 : (block + 1) * 384], NN
            ).astype(BF)

    def coarse_backward(h):
        cols_h = slice(h * DH, (h + 1) * DH)
        go = do_c[:, cols_h]
        gof = go.astype(F32)
        delta = jnp.sum(gof * attn_all[FR:R, cols_h].astype(F32), axis=1, keepdims=True)
        gcn[:, cols_h] = (gof * inverse_c[h]).astype(BF)
        dp = dot(go, cv[:, cols_h], NT)
        eb = jnp.concatenate([ecds[h, 0, 0], ecds[h, 1, 0]], axis=1)
        ds = (eb.astype(F32) * ((dp - delta) * (inverse_c[h] * factor))).astype(BF)
        for i in range(2):
            ecds[h, i, 1] = ds[:, HALF * i : HALF * (i + 1)]
        cbuf[core, z, xh, CR : 2 * CR, cols_h] = dot(ds, ck[:, cols_h], NN).astype(BF)

    def backward(h):
        cols_h = slice(h * DH, (h + 1) * DH)
        go = do2[:, cols_h]
        gof = go.astype(F32)
        attn = jnp.concatenate([attn_all[0:FR, cols_h], attn_all[R : R + FR, cols_h]], axis=0)
        delta = jnp.sum(gof * attn.astype(F32), axis=1, keepdims=True)
        c = inverse[h] * factor
        go_n = (gof * inverse[h]).T.astype(BF)
        q_t = q2[h].astype(F32).T.astype(BF)
        dq = jnp.zeros((2 * FR, DH), F32)
        for j, cols in enumerate(blocks):
            dp = dot(go, value_block(h, j), NT)
            eb = ebuf[h, :, cols]
            ds = (eb.astype(F32) * ((dp - delta) * c)).astype(BF)
            dq = dq + dot(ds, key_block(h, j), NN)
            dk_t = dot(q_t, ds, NN)
            dv_t = dot(go_n, eb, NN)
            if j == 0:
                c_e = jnp.concatenate([ecds[h, xh, 0], ecx[h, 0]], axis=0)
                c_ds = jnp.concatenate([ecds[h, xh, 1], ecx[h, 1]], axis=0)
                c_go = jnp.concatenate([gcn[:, cols_h], gcx[:, cols_h]], axis=0)
                dk = (dk_t.T + dot(c_ds, qc[h], TN)).astype(BF)
                dv = (dv_t.T + dot(c_e, c_go, TN)).astype(BF)
                for r in range(4):
                    for cx in range(2):
                        at = (r * 2 + cx) * CR
                        pa[h, cx, r, 256:288, :] = dk[at : at + CR]
                        pa[h, cx, r, 288:320, :] = dv[at : at + CR]
            else:
                dk_t, dv_t = dk_t.astype(BF), dv_t.astype(BF)
                for r in range(4):
                    pa[h, planes[j - 1], r, 0:128, :] = dk_t[:, 128 * r : 128 * r + 128]
                    pa[h, planes[j - 1], r, 128:256, :] = dv_t[:, 128 * r : 128 * r + 128]
            yield
        fdq_own[h] = dq[0:FR]
        dq_s[:, cols_h] = dq[FR:].astype(BF)

    fdq_own = [None] * HL

    def up(value):
        return value.astype(F32)

    class RingFirst:
        def __init__(self, mine, from_ring, from_pair, rings, ring, pair, ids, pair_id):
            self.mine, self.from_ring, self.from_pair = mine, from_ring, from_pair
            self.rings, self.ring, self.pair, self.ids, self.pair_id = rings, ring, pair, ids, pair_id

        def b(self):
            self.cr = [
                send(self.mine.at[r], self.from_ring.at[i], self.ids[i]) for i, r in enumerate(self.rings)
            ]

        def c(self):
            for copy in self.cr:
                copy.wait_recv()

            def total(p):
                value = up(self.mine[self.ring, p])
                for i in range(3):
                    value = value + up(self.from_ring[i, p])
                return value

            self.mine[self.ring, 1 - self.pair] = total(1 - self.pair).astype(BF)
            self.cx = send(self.mine.at[self.ring, 1 - self.pair], self.from_pair, self.pair_id)
            self.kept = total(self.pair)

        def d(self):
            self.cx.wait_recv()
            return self.kept + up(self.from_pair[...])

    class RingOnly:
        def __init__(self, src, from_sib, from_ring):
            self.src, self.from_sib, self.from_ring = src, from_sib, from_ring

        def a(self):
            self.cs = send(self.src[0], self.from_sib, sib)

        def b(self):
            mine = self.src[1]
            self.cs.wait_recv()
            self.cr = []
            for i, r in enumerate(rings):
                mine[r] = (up(mine[r]) + up(self.from_sib[r])).astype(BF)
                self.cr.append(send(mine.at[r], self.from_ring.at[i], pz[i]))
            self.kept = up(mine[z]) + up(self.from_sib[z])

        def d(self):
            value = self.kept
            for i in range(3):
                self.cr[i].wait_recv()
                value = value + up(self.from_ring[i])
            return value

    class PairFirst:
        def __init__(self, src, from_sib, from_ring, from_pair):
            self.src, self.from_sib, self.from_ring, self.from_pair = src, from_sib, from_ring, from_pair

        def a(self):
            self.cs = send(self.src[0], self.from_sib, sib)

        def b(self):
            mine = self.src[1]
            self.cs.wait_recv()
            p = 1 - xh
            for r in range(4):
                mine[r, p] = (up(mine[r, p]) + up(self.from_sib[r, p])).astype(BF)
            self.cx = send(mine.at[:, p], self.from_pair, px)

        def c(self):
            mine = self.src[1]
            self.cx.wait_recv()

            def total(r):
                return up(mine[r, xh]) + up(self.from_sib[r, xh]) + up(self.from_pair[r])

            self.cr = []
            for i, r in enumerate(rings):
                mine[r, xh] = total(r).astype(BF)
                self.cr.append(send(mine.at[r, xh], self.from_ring.at[i], pz[i]))
            self.kept = total(z)

        def d(self):
            value = self.kept
            for i in range(3):
                self.cr[i].wait_recv()
                value = value + up(self.from_ring[i])
            return value

    class RingPair:
        def __init__(self, src, from_sib, from_ring, from_pair):
            self.src, self.from_sib, self.from_ring, self.from_pair = src, from_sib, from_ring, from_pair

        def a(self):
            self.cs = send(self.src[0], self.from_sib, sib)

        def b(self):
            mine = self.src[1]
            self.cs.wait_recv()
            self.cr = []
            for i, r in enumerate(rings):
                mine[r] = (up(mine[r]) + up(self.from_sib[r])).astype(BF)
                self.cr.append(send(mine.at[r], self.from_ring.at[i], pz[i]))

        def c(self):
            mine = self.src[1]
            for copy in self.cr:
                copy.wait_recv()

            def total(p):
                value = up(mine[z, p]) + up(self.from_sib[z, p])
                for i in range(3):
                    value = value + up(self.from_ring[i, p])
                return value

            mine[z, 1 - xh] = total(1 - xh).astype(BF)
            self.cx = send(mine.at[z, 1 - xh], self.from_pair, px)
            self.kept = total(xh)

        def d(self):
            self.cx.wait_recv()
            return self.kept + up(self.from_pair[...])

    sums_a = [RingOnly((pa.at[h, 1 - core], pa.at[h, core]), sa.at[h], az.at[h]) for h in range(HL)]
    sums_w = [
        RingPair((pw.at[h, 1 - core], pw.at[h, core]), sw.at[h], wz.at[h], wx.at[h, 0])
        if h < 2
        else PairFirst((pw.at[h, 1 - core], pw.at[h, core]), sw.at[h], wz.at[h, :, 0], wx.at[h])
        for h in range(HL)
    ]
    coarse_sum = RingFirst(oc, ocr, ocx, (y2, y1, y3), y, xl, py, pxl)
    fine_sum = RingFirst(of, ofr, ofx, (y2, y1, y3), y, xl, py, pxl)

    out_copies = []

    def store(src, dst):
        copy = pltpu.make_async_copy(src, dst, osem.at[len(out_copies)])
        out_copies.append(copy)
        copy.start()

    lane = lax.broadcasted_iota(jnp.int32, (192, 128), 1)

    def finish_a(h):
        total = sums_a[h].d()
        cols_h = slice(h * DH, (h + 1) * DH)
        fdk[:, cols_h] = total[0:128].T.astype(BF)
        fdv[:, cols_h] = total[128:256].T.astype(BF)
        cdk[:, cols_h] = total[256:288].astype(BF)
        cdv[:, cols_h] = total[288:320].astype(BF)

    def finish_w(h):
        total = sums_w[h].d()
        for i in range(3):
            piece = total[64 * i : 64 * i + 64]
            wsend[h, 128 * i : 128 * i + 128, :] = jnp.concatenate([piece, piece], axis=0).T
        other = pl.ds(pl.multiple_of((1 - core) * 192, 64), 192)
        return send(wsend.at[h, other], wrecv.at[h], sib)

    def finish_weight(h, copy):
        copy.wait_recv()
        mine = wsend[h, pl.ds(pl.multiple_of(core * 192, 64), 192), :]
        wg[:, h * DH : (h + 1) * DH] = jnp.where((lane < 64) == (core == 0), mine, wrecv[h])

    def coarse_done():
        cbuf[core, z, xh, 0:CR, :] = coarse_sum.d().astype(BF)
        coarse_gather.a()

    def fine_done():
        fout[...] = fine_sum.d().astype(BF)
        store(fout, fout_o)

    def run(steps, events=()):
        todo = list(events)
        for i, _ in enumerate(steps):
            while todo and todo[0][0] <= i:
                todo.pop(0)[1]()
        for _, event in todo:
            event()

    g, A, W = gathers, sums_a, sums_w
    in_ck.wait()
    in_cv.wait()
    for h in range(HL):
        coarse_forward(h)
    gather_a(1)
    cot_gather.b()
    gather_a(2)
    in_w.wait()
    coarse_project()
    coarse_sum.b()
    g[0].d()
    c_scale.wait_recv()
    row_scale[0] = jnp.concatenate([fsc_col, column(scx[...].astype(F32)[0:1])], axis=0)
    c_query.wait_recv()
    g[0].e()
    for i in range(2):
        for r in range(4):
            at = (4 * i + r) * 128
            ksc[:, at : at + 128] = kv[0, planes[i], r, 256:272, :].astype(F32)[0:8]
    x0 = forward(0)
    g[1].d()
    g[1].e()
    x1 = forward(1)
    g[2].d()
    g[2].e()
    x2 = forward(2)
    cot_gather.d()
    c_do = [grad_attn(h) for h in range(HL)]
    for h in range(HL):
        coarse_backward(h)
    c_ec = send(ecds.at[:, 1 - xh], ecx, px)
    c_gc = send(gcn, gcx, px)
    combine(0, x0)
    weight_grad(0)
    W[0].a()
    combine(1, x1)
    weight_grad(1)
    W[1].a()
    W[0].b()
    coarse_sum.c()
    c_do[0].wait_recv()
    c_ec.wait_recv()
    c_gc.wait_recv()
    coarse_done()
    run(backward(0), [(1, A[0].a)])
    W[1].b()
    combine(2, x2)
    weight_grad(2)
    W[2].a()
    fine_project()
    fine_sum.b()
    A[0].b()
    c_do[1].wait_recv()
    run(backward(1), [(1, A[1].a)])
    W[2].b()
    coarse_gather.b()
    A[1].b()
    W[0].c()
    c_do[2].wait_recv()
    run(backward(2), [(1, A[2].a)])
    c_dq = send(dq_s, dq_r, px)
    A[2].b()
    W[1].c()
    finish_a(0)
    W[2].c()
    c_w0 = finish_w(0)
    finish_a(1)
    c_w1 = finish_w(1)
    coarse_gather.d()
    fine_sum.c()
    c_dq.wait_recv()
    for h in range(HL):
        cols_h = slice(h * DH, (h + 1) * DH)
        fdq[:, cols_h] = (fdq_own[h] + up(dq_r[:, cols_h])).astype(BF)
    store(fdq, fdq_o)
    finish_a(2)
    store(fdk, fdk_o)
    store(fdv, fdv_o)
    store(cdk, cdk_o)
    store(cdv, cdv_o)
    c_w2 = finish_w(2)
    finish_weight(0, c_w0)
    finish_weight(1, c_w1)
    coarse_gather.e()
    store(cbuf, cbuf_o)
    fine_done()
    finish_weight(2, c_w2)
    store(wg, wg_o)
    for copy in started:
        copy.wait_send()
    for copy in out_copies:
        copy.wait()


def place(fout, fdq, fdk, fdv, cdk, cdv, wg, cbuf, *rest):
    outs, held, sem_in, sem_out = rest[:9], rest[9:18], rest[18], rest[19]
    loads = [[] for _ in outs]
    for i, src in ((1, fout), (3, cdk), (4, cdv), (5, fdq), (6, fdk), (7, fdv), (8, wg)):
        loads[i].append((src, held[i]))
    for core in range(2):
        for xh in range(2):
            loads[0].append((cbuf.at[core, :, xh, pl.ds(0, CR)], held[0].at[xh, :, core]))
            loads[2].append((cbuf.at[core, :, xh, pl.ds(CR, CR)], held[2].at[xh, :, core]))
    order = (0, 2, 8, 1, 5, 6, 7, 3, 4)
    copies = {}
    count = 0
    for i in order:
        copies[i] = []
        for src, dst in loads[i]:
            copies[i].append(pltpu.make_async_copy(src, dst, sem_in.at[count]))
            copies[i][-1].start()
            count += 1
    stores = []
    for i in order:
        for copy in copies[i]:
            copy.wait()
        stores.append(pltpu.make_async_copy(held[i], outs[i], sem_out.at[i]))
        stores[-1].start()
    for copy in stores:
        copy.wait()


def on_device(cq, ck, cv, fq, fk, fv, csz, fsz, fpos, w, cc, fc):
    vmem = pl.BlockSpec(memory_space=pltpu.VMEM)
    smem = pl.BlockSpec(memory_space=pltpu.SMEM)
    hbm = pl.BlockSpec(memory_space=pl.ANY)
    shapes = [
        ((128, 384), BF), ((128, 384), BF), ((128, 384), BF), ((128, 384), BF), ((32, 384), BF),
        ((32, 384), BF), ((192, 384), F32), ((2, 4, 2, 2 * CR, 384), BF),
    ]
    v = pltpu.VMEM
    raw = pl.pallas_call(
        kernel,
        out_shape=[jax.ShapeDtypeStruct(s, d) for s, d in shapes],
        in_specs=[hbm] * 6 + [smem] * 2 + [vmem] + [hbm] * 3,
        out_specs=[hbm] * 8,
        scratch_shapes=[
            v((512, 384), BF),
            v((512, 384), BF),
            v((384, 3072), BF),
            v((HL, 2 * FR, DH), BF),
            v((HL, 2 * CR, DH), BF),
            v((HL, 2, 4, KR, DH), BF),
            v((4, 2, R, 384), BF),
            v((16, DH), BF),
            v((8, 1024), F32),
            v((HL, 2 * FR, 1280), F32),
            v((HL, 2 * FR, 1280), BF),
            v((HL, 2, 2, CR, HALF), BF),
            v((HL, 2, CR, HALF), BF),
            v((2 * R, 384), BF),
            v((CR, 384), BF),
            v((CR, 384), BF),
            v((CR, 384), BF),
            v((2 * FR, 384), BF),
            v((HL, 2 * FR, DH), BF),
            v((HL, 2 * FR, DH), BF),
            v((HL, 8, 2 * FR), F32),
            v((HL, 8, 2 * FR), F32),
            v((FR, 384), BF),
            v((FR, 384), BF),
            v((HL, 2, 4, CA, DH), BF),
            v((HL, 2, 4, 2, CW, DH), BF),
            v((HL, 4, CA, DH), BF),
            v((HL, 4, 2, CW, DH), BF),
            v((HL, 3, CA, DH), BF),
            v((HL, 3, 2, CW, DH), BF),
            v((HL, 4, CW, DH), BF),
            v((4, 2, CR, 384), BF),
            v((3, 2, CR, 384), BF),
            v((CR, 384), BF),
            v((4, 2, FR, 384), BF),
            v((3, 2, FR, 384), BF),
            v((FR, 384), BF),
            v((2, 4, 2, 2 * CR, 384), BF),
            v((HL, 384, 128), F32),
            v((HL, 192, 128), F32),
            v((128, 384), BF),
            v((128, 384), BF),
            v((128, 384), BF),
            v((128, 384), BF),
            v((32, 384), BF),
            v((32, 384), BF),
            v((192, 384), F32),
            pltpu.SemaphoreType.DMA((96,)),
            pltpu.SemaphoreType.DMA((96,)),
            pltpu.SemaphoreType.DMA((24,)),
            pltpu.SemaphoreType.DMA((9,)),
        ],
        compiler_params=pltpu.CompilerParams(
            collective_id=0, has_side_effects=True, vmem_limit_bytes=56 * 2**20
        ),
        cost_estimate=pl.CostEstimate(flops=7 * 10**9, bytes_accessed=8 * 10**6, transcendentals=1300000),
    )(cq, ck, cv, fq, fk, fv, csz, fsz, fpos.reshape(1, 128), w, cc, fc)
    coarse = ((2, 4, 2, CR, 384), BF)
    fine = ((128, 384), BF)
    small = ((32, 384), BF)
    placed = [coarse, fine, coarse, small, small, fine, fine, fine, ((192, 384), F32)]
    outs = pl.pallas_call(
        place,
        out_shape=[jax.ShapeDtypeStruct(s, d) for s, d in placed],
        in_specs=[hbm] * 8,
        out_specs=[hbm] * 9,
        scratch_shapes=[pltpu.VMEM(s, d) for s, d in placed]
        + [pltpu.SemaphoreType.DMA((15,)), pltpu.SemaphoreType.DMA((9,))],
    )(*raw)
    outs = list(outs)
    outs[0] = outs[0].reshape(512, 384)
    outs[2] = outs[2].reshape(512, 384)
    outs[8] = outs[8].T
    return tuple(outs)


def solution(mesh):
    placed = (
        P(None, "head"), P(None, "head"), P(None, "head"),
        P("ctx", "head"), P("ctx", "head"), P("ctx", "head"),
        P(), P(), P("ctx"), P("head", None), P(None, "head"), P("ctx", "head"),
    )
    return jax.shard_map(
        on_device,
        mesh=mesh,
        in_specs=placed,
        out_specs=(
            P(None, "head"), P("ctx", "head"), P(None, "head"),
            P("ctx", "head"), P("ctx", "head"), P("ctx", "head"),
            P("ctx", "head"), P("ctx", "head"), P("head", "ctx"),
        ),
        check_vma=False,
    )
```
